32 devices in a mesh: groups: 2 (over x), orb: 16 (over z, y, core).
Axes of the slice: x: 2, y: 2, z: 4, core: 2. Of those that a mesh axis runs over, the one named last changes fastest.
Arguments:
- orbitals: bfloat16 [8192, 4096], P('orb', 'groups'), parts along dimension 1, may hold values from -6 to 6
- dipole_blocks: bfloat16 [6, 64, 3, 128, 128], P('groups', 'orb'), parts along dimension 0, may hold values from -0.3125 to 0.3125
- coupling_mask: int32 [64, 4], P('orb', 'groups'), parts along dimension 1, may hold values 0 or 1
- matchings: int32 [4, 16], P('groups'), parts along dimension 0, may hold values from 0 to 15, each once within a row
Outputs:
- localized: bfloat16 [8192, 4096], P('orb', 'groups'), parts along dimension 1
The draws below stay inside these ranges and needn't reach their ends.
There are 2 independent parts, one for each index of `groups`. The reference program is written for one: setup_inputs(seed, part) draws one part's arguments, and reference() takes and returns one part's arrays. A program takes and returns all parts, laid end to end along the dimension named above; each array names one. Nothing has to cross between parts.
All inputs are finite; a program needn't handle non-finite values. No bound on the sum of `coupling_mask` on one device may be relied on, other than what follows from the above.
Results may differ from the reference program's by a relative error of at most 0.012.
The reference program's roundings to bfloat16 on the way (of `images` and `rotation`) count: a program that leaves them out, or rounds other values in their place, can miss the bound.
Values may be sent and summed in bfloat16 or wider, within the bound.
No kernel may reach another device: no remote copies, remote signals or barrier semaphores. Data moves between devices by JAX's collectives and lax.ppermute only.
A program may use at most 128 MiB of HBM per device.

```python
import jax
import jax.numpy as jnp
from jax import lax

NORB = 2048
HALF = 128
BLK = 128
ROUNDS = 2
NBAS = 8192
NBLOCKS = 64
NBLK = 16


def place_ends(result, own_key, least, top_value):
    spot = [jax.random.randint(jax.random.fold_in(own_key, axis), (), 0, length) for axis, length in enumerate(result.shape)]
    main_axis = result.shape.index(max(result.shape))
    neighbour = spot[:main_axis] + [(spot[main_axis] + 1) % result.shape[main_axis]] + spot[main_axis + 1:]
    return result.at[tuple(spot)].set(least).at[tuple(neighbour)].set(top_value)


def block_scale(own_key, dims, shards, low, top_value):
    def one(dim, shards_of):
        draws = jax.random.uniform(jax.random.fold_in(jax.random.fold_in(own_key, 6), dim), (shards_of,), jnp.float32, low / len(shards), top_value / len(shards))
        return jnp.repeat(jnp.exp(draws), dims[dim] // shards_of).reshape((-1,) + (1,) * (len(dims) - dim - 1))

    level = one(*shards[0])
    for cut in shards[1:]:
        level = level * one(*cut)
    return level


def centred(own_key, dims, scale, reach, pieces=(), kind=jnp.bfloat16):
    array = scale * jax.random.normal(own_key, dims, jnp.float32)
    if pieces:
        array = array * block_scale(own_key, dims, pieces, -0.22, 0.18)
    return jnp.clip(array, -reach, reach).astype(kind)


def setup_inputs(seed: int = 0, part: int = 0) -> dict:
    key_list = jax.random.split(jax.random.key(seed), 5)
    own_keys = jax.random.split(jax.random.fold_in(key_list[4], part), 5)
    return {
        "orbitals": centred(own_keys[0], (NBAS, NORB), 1.0, 6.0, ((0, 16),)),
        "dipole_blocks": centred(own_keys[1], (3, NBLOCKS, 3, BLK, BLK), (3 * BLK) ** -0.5, 0.3125, ((1, 16),)),
        "coupling_mask": place_ends((jax.random.randint(own_keys[2], (NBLOCKS, 2), 0, 2) < 1).astype(jnp.int32), jax.random.fold_in(own_keys[2], 1), 0, 1),
        "matchings": jax.vmap(lambda own: jax.random.permutation(own, NBLK))(jax.random.split(own_keys[3], ROUNDS)).reshape((ROUNDS, NBLK)).astype(jnp.int32),
    }


def cayley(generator):
    identity = jnp.eye(generator.shape[-1], dtype=jnp.float32)
    square = jnp.matmul(generator, generator, precision=lax.Precision.HIGHEST)
    factor = jnp.linalg.cholesky(identity - 0.25 * square)
    raised = identity + 0.5 * generator
    numerator = jnp.matmul(raised, raised, precision=lax.Precision.HIGHEST)

    def solve_one(chol_factor, target):
        return jax.scipy.linalg.cho_solve((chol_factor, True), target)
    return jax.vmap(solve_one)(factor, numerator)

def reference(orbitals, dipole_blocks, coupling_mask, matchings):
    basis_count, orb_count = orbitals.shape
    block_rows = basis_count // BLK
    block_count = orb_count // HALF
    pair_count = orb_count // (2 * HALF)
    pair_width = 2 * HALF
    padded = jnp.pad(orbitals, ((BLK, BLK), (0, 0)))
    mask_full = jnp.stack([coupling_mask[:, 0], jnp.ones((block_rows,), jnp.int32), coupling_mask[:, 1]], axis=1).astype(jnp.float32)
    image_list = []
    for component in range(3):
        summed = jnp.zeros((block_rows, BLK, orb_count), jnp.float32)
        for offset in range(3):
            shifted = padded[offset * BLK:offset * BLK + basis_count].reshape(block_rows, BLK, orb_count).astype(jnp.float32)
            blocks = dipole_blocks[component, :, offset].astype(jnp.float32) * mask_full[:, offset][:, None, None]
            summed = summed + jnp.einsum('bij,bjn->bin', blocks, shifted, precision=lax.Precision.HIGHEST)
        image_list.append(summed.reshape(basis_count, orb_count).astype(jnp.bfloat16))
    images = jnp.stack(image_list)
    current = orbitals
    for round_index in range(ROUNDS):
        matching = matchings[round_index].astype(jnp.int32)
        inverse = jnp.argsort(matching).astype(jnp.int32)
        cols_now = jnp.take(current.reshape(basis_count, block_count, HALF), matching, axis=1).reshape(basis_count, pair_count, pair_width)
        image_now = jnp.take(images.reshape(3, basis_count, block_count, HALF), matching, axis=2).reshape(3, basis_count, pair_count, pair_width)
        pair_mats = jnp.einsum('rpa,krpb->pkab', cols_now.astype(jnp.float32), image_now.astype(jnp.float32), precision=lax.Precision.HIGHEST)
        diagonal = jnp.diagonal(pair_mats, axis1=2, axis2=3)
        weighted = jnp.sum(pair_mats * (diagonal[:, :, :, None] - diagonal[:, :, None, :]), axis=1)
        gradient = weighted - jnp.swapaxes(weighted, 1, 2)
        rotation = cayley(0.02 / basis_count * gradient).astype(jnp.bfloat16)
        rotated = jnp.einsum('rpa,pab->rpb', cols_now.astype(jnp.float32), rotation.astype(jnp.float32), precision=lax.Precision.HIGHEST).astype(jnp.bfloat16)
        current = jnp.take(rotated.reshape(basis_count, block_count, HALF), inverse, axis=1).reshape(basis_count, orb_count)
        if round_index + 1 < ROUNDS:
            image_rot = jnp.einsum('krpa,pab->krpb', image_now.astype(jnp.float32), rotation.astype(jnp.float32), precision=lax.Precision.HIGHEST).astype(jnp.bfloat16)
            images = jnp.take(image_rot.reshape(3, basis_count, block_count, HALF), inverse, axis=2).reshape(3, basis_count, orb_count)
    return current
```

```python
import functools

import jax
import jax.numpy as jnp
from jax import lax
from jax.experimental import pallas as pl
from jax.experimental.pallas import tpu as pltpu
from jax.sharding import PartitionSpec as P

HALF = 128
BLK = 128
ROUNDS = 2
PAIR = 2 * HALF
F32 = jnp.float32
BF16 = jnp.bfloat16
WIRE = jnp.float32
VMEM_LIMIT = 32 * 1024 * 1024


def params():
    return pltpu.CompilerParams(vmem_limit_bytes=VMEM_LIMIT)


def bits_of(count):
    return count.bit_length() - 1


def bitrev(value, bits):
    return sum(((value >> j) & 1) << (bits - 1 - j) for j in range(bits))


def swap(block, distance):
    count = lax.axis_size("orb")
    return lax.ppermute(block, "orb", [(i, i ^ distance) for i in range(count)])


def put_diag(diag_ref, component, block, cols, image, first):
    total = jnp.sum(cols.astype(F32) * image.astype(F32), axis=0, keepdims=True)
    for half in range(total.shape[1] // HALF):
        spot = pl.ds(block + half, 1)
        piece = total[:, half * HALF : (half + 1) * HALF]
        if first:
            diag_ref[component, spot, :] = piece
        else:
            diag_ref[component, spot, :] += piece


def inner_kernel(block_rows, blocks_ref, cols_ref, image_ref, diag_ref):
    step = pl.program_id(0)
    for b in range(1, block_rows - 1):
        out = jnp.dot(
            blocks_ref[b], cols_ref[(b - 1) * BLK : (b + 2) * BLK], preferred_element_type=F32
        ).astype(BF16)
        own = cols_ref[b * BLK : (b + 1) * BLK]
        for k in range(3):
            image = out[k * BLK : (k + 1) * BLK]
            image_ref[k, (b - 1) * BLK : b * BLK] = image
            put_diag(diag_ref, k, 2 * step, own, image, b == 1)


def inner_images(blocks, orbitals):
    row_count, orb_count = orbitals.shape
    block_rows = row_count // BLK
    inner = row_count - 2 * BLK
    return pl.pallas_call(
        functools.partial(inner_kernel, block_rows),
        out_shape=(
            jax.ShapeDtypeStruct((3, inner, orb_count), BF16),
            jax.ShapeDtypeStruct((3, orb_count // HALF, HALF), F32),
        ),
        grid=(orb_count // PAIR,),
        in_specs=[
            pl.BlockSpec(blocks.shape, lambda c: (0, 0, 0)),
            pl.BlockSpec((row_count, PAIR), lambda c: (0, c)),
        ],
        out_specs=(
            pl.BlockSpec((3, inner, PAIR), lambda c: (0, 0, c)),
            pl.BlockSpec((3, orb_count // HALF, HALF), lambda c: (0, 0, 0)),
        ),
        compiler_params=params(),
        name="inner_images",
    )(blocks, orbitals)


def edge_kernel(block_rows, blocks_ref, cols_ref, low_ref, high_ref, start_ref, image_ref, diag_ref):
    step = pl.program_id(0)

    @pl.when(step == 0)
    def _():
        diag_ref[...] = start_ref[...]

    for place, b in ((0, 0), (1, block_rows - 1)):
        if b == 0:
            window = jnp.concatenate([low_ref[...], cols_ref[: 2 * BLK]], axis=0)
        else:
            window = jnp.concatenate([cols_ref[(b - 1) * BLK :], high_ref[...]], axis=0)
        out = jnp.dot(blocks_ref[b], window, preferred_element_type=F32).astype(BF16)
        own = cols_ref[b * BLK : (b + 1) * BLK]
        for k in range(3):
            image = out[k * BLK : (k + 1) * BLK]
            image_ref[k, place * BLK : (place + 1) * BLK] = image
            put_diag(diag_ref, k, 2 * step, own, image, False)


def edge_images(blocks, orbitals, low, high, start):
    row_count, orb_count = orbitals.shape
    block_rows = row_count // BLK
    return pl.pallas_call(
        functools.partial(edge_kernel, block_rows),
        out_shape=(
            jax.ShapeDtypeStruct((3, 2 * BLK, orb_count), BF16),
            jax.ShapeDtypeStruct((3, orb_count // HALF, HALF), F32),
        ),
        grid=(orb_count // PAIR,),
        in_specs=[
            pl.BlockSpec(blocks.shape, lambda c: (0, 0, 0)),
            pl.BlockSpec((row_count, PAIR), lambda c: (0, c)),
            pl.BlockSpec((BLK, PAIR), lambda c: (0, c)),
            pl.BlockSpec((BLK, PAIR), lambda c: (0, c)),
            pl.BlockSpec(start.shape, lambda c: (0, 0, 0)),
        ],
        out_specs=(
            pl.BlockSpec((3, 2 * BLK, PAIR), lambda c: (0, 0, c)),
            pl.BlockSpec((3, orb_count // HALF, HALF), lambda c: (0, 0, 0)),
        ),
        compiler_params=params(),
        name="edge_images",
    )(blocks, orbitals, low, high, start)


def lower_mask():
    rows = lax.broadcasted_iota(jnp.int32, (HALF, HALF), 0)
    cols = lax.broadcasted_iota(jnp.int32, (HALF, HALF), 1)
    return rows > cols


def whole_image(refs, component):
    pieces = [
        jnp.concatenate([refs[i][component], refs[i + 1][component]], axis=1)
        for i in range(0, len(refs), 2)
    ]
    if len(pieces) == 1:
        return pieces[0]
    inner, edge = pieces
    return jnp.concatenate([edge[:BLK], inner, edge[BLK:]], axis=0)


def gram_kernel(place_ref, *refs):
    ins, sums_ref = refs[:-1], refs[-1]
    cols = jnp.concatenate([ins[0][...], ins[1][...]], axis=1)
    low = lower_mask()
    for k in range(3):
        image = whole_image(ins[2:], k)
        mat = lax.dot_general(
            cols, image, (((0,), (0,)), ((), ())), preferred_element_type=F32
        )
        both = mat + mat.T
        sums_ref[0, k, :HALF] = both[:HALF, HALF:]
        sums_ref[0, k, HALF:] = jnp.where(low, both[:HALF, :HALF], both[HALF:, HALF:])


def pair_sums(place, cols, images):
    row_count, orb_count = cols.shape
    pair_count = orb_count // PAIR
    specs = [
        pl.BlockSpec((row_count, HALF), lambda p, at, h=h: (0, at[2 * p + h])) for h in (0, 1)
    ]
    operands = [cols, cols]
    for image in images:
        for h in (0, 1):
            specs.append(
                pl.BlockSpec(
                    (3, image.shape[1], HALF), lambda p, at, h=h: (0, 0, at[2 * p + h])
                )
            )
            operands.append(image)
    return pl.pallas_call(
        gram_kernel,
        out_shape=jax.ShapeDtypeStruct((pair_count, 3, PAIR, HALF), F32),
        grid_spec=pltpu.PrefetchScalarGridSpec(
            num_scalar_prefetch=1,
            grid=(pair_count,),
            in_specs=specs,
            out_specs=pl.BlockSpec((1, 3, PAIR, HALF), lambda p, at: (p, 0, 0, 0)),
        ),
        compiler_params=params(),
        name="pair_sums",
    )(place, *operands)


def weight_kernel(place_ref, me_ref, sums_ref, diag_ref, keep_ref, send_ref):
    p = pl.program_id(0)
    core = me_ref[0] & 1
    low = lower_mask()
    rows = [
        diag_ref[k, pl.ds(place_ref[2 * p + h], 1), :] for k in range(3) for h in (0, 1)
    ]
    turned = jnp.concatenate(rows + rows[:2], axis=0).T
    cross = jnp.zeros((HALF, HALF), F32)
    within = jnp.zeros((HALF, HALF), F32)
    for k in range(3):
        first_col = turned[:, 2 * k : 2 * k + 1]
        second_col = turned[:, 2 * k + 1 : 2 * k + 2]
        first_row, second_row = rows[2 * k], rows[2 * k + 1]
        cross += sums_ref[0, k, :HALF] * (first_col - second_row)
        within += sums_ref[0, k, HALF:] * (
            jnp.where(low, first_col, second_col) - jnp.where(low, first_row, second_row)
        )
    mine = core == 0
    keep_ref[0] = jnp.where(mine, cross, within)
    send_ref[0] = jnp.where(mine, within, cross)


def weigh(place, me, sums, diag):
    pair_count = sums.shape[0]
    tile = pl.BlockSpec((1, HALF, HALF), lambda p, at, who: (p, 0, 0))
    shape = jax.ShapeDtypeStruct((pair_count, HALF, HALF), F32)
    return pl.pallas_call(
        weight_kernel,
        out_shape=(shape, shape),
        grid_spec=pltpu.PrefetchScalarGridSpec(
            num_scalar_prefetch=2,
            grid=(pair_count,),
            in_specs=[
                pl.BlockSpec((1, 3, PAIR, HALF), lambda p, at, who: (p, 0, 0, 0)),
                pl.BlockSpec(diag.shape, lambda p, at, who: (0, 0, 0)),
            ],
            out_specs=(tile, tile),
        ),
        compiler_params=params(),
        name="weigh",
    )(place, me, sums, diag)


def matmul(left, right):
    return jnp.dot(left, right, precision=lax.Precision.HIGHEST, preferred_element_type=F32)


def rotation_kernel(scale, subs, me_ref, packed_ref, out_ref, sum_ref, power_ref):
    sub = me_ref[0] & (subs - 1)
    pieces = [packed_ref[bitrev(i, bits_of(subs)) ^ sub] for i in range(subs)]
    packed = jnp.concatenate(pieces, axis=0) * scale
    cross, within = packed[:HALF], packed[HALF:]
    low = lower_mask()
    first = jnp.where(low, within, 0.0)
    second = jnp.where(low, 0.0, within)
    half_gen = jnp.concatenate(
        [
            jnp.concatenate([first - first.T, cross], axis=1),
            jnp.concatenate([-cross.T, second - second.T], axis=1),
        ],
        axis=0,
    )
    rows = lax.broadcasted_iota(jnp.int32, (PAIR, PAIR), 0)
    cols = lax.broadcasted_iota(jnp.int32, (PAIR, PAIR), 1)
    eye = jnp.where(rows == cols, 1.0, 0.0).astype(F32)
    square = -matmul(half_gen, half_gen)
    fourth = matmul(square, square)
    bound = 1.0001 * jnp.sqrt(jnp.max(jnp.sum(jnp.abs(fourth), axis=1)))
    factor = 2.0 / (2.0 + bound)
    rest = 1.0 - factor
    sum_ref[...] = factor * ((1.0 + rest) * eye - factor * square)
    power_ref[...] = rest * rest * eye - (2.0 * rest * factor) * square + factor * factor * fourth

    def going(state):
        step, left = state
        return jnp.logical_and(step < 24, left > 1e-8)

    def body(state):
        step, left = state
        power = power_ref[...]
        sum_ref[...] += matmul(sum_ref[...], power)
        power_ref[...] = matmul(power, power)
        return step + 1, left * left

    reach = bound / (2.0 + bound)
    lax.while_loop(going, body, (jnp.int32(0), reach * reach))
    result = 2.0 * matmul(eye + half_gen, sum_ref[...]) - eye
    share = PAIR // subs
    for i in range(subs):

        @pl.when(sub == i)
        def _():
            out_ref[...] = result[i * share : (i + 1) * share].astype(BF16)


def rotation_share(scale, me, packed):
    subs = packed.shape[0]
    return pl.pallas_call(
        functools.partial(rotation_kernel, scale, subs),
        out_shape=jax.ShapeDtypeStruct((PAIR // subs, PAIR), BF16),
        grid_spec=pltpu.PrefetchScalarGridSpec(
            num_scalar_prefetch=1,
            grid=(1,),
            in_specs=[pl.BlockSpec(packed.shape, lambda i, who: (0, 0, 0))],
            out_specs=pl.BlockSpec((PAIR // subs, PAIR), lambda i, who: (0, 0)),
            scratch_shapes=[pltpu.VMEM((PAIR, PAIR), F32), pltpu.VMEM((PAIR, PAIR), F32)],
        ),
        compiler_params=params(),
        name="rotation",
    )(me, packed)


def assemble(gathered_ref, me, pair_count, pair):
    subs = PAIR // gathered_ref.shape[1]
    my_sub, my_pair = me & (subs - 1), me // subs
    return jnp.concatenate(
        [gathered_ref[(i ^ my_sub) * pair_count + (pair ^ my_pair)] for i in range(subs)], axis=0
    )


def rotate_kernel(pair_count, place_ref, me_ref, *refs):
    ins, (gathered_ref, out_ref, image_ref, diag_ref) = refs[:-4], refs[-4:]
    p = pl.program_id(0)
    rotation = assemble(gathered_ref, me_ref[0], pair_count, p)
    cols = jnp.concatenate([ins[0][...], ins[1][...]], axis=1)
    turned = jnp.dot(cols, rotation, preferred_element_type=F32).astype(BF16)
    out_ref[...] = turned
    for k in range(3):
        image = whole_image(ins[2:], k)
        moved = jnp.dot(image, rotation, preferred_element_type=F32).astype(BF16)
        image_ref[k] = moved
        put_diag(diag_ref, k, 2 * p, turned, moved, True)


def rotate(place, me, cols, images, gathered):
    row_count, orb_count = cols.shape
    pair_count = orb_count // PAIR
    specs = [
        pl.BlockSpec((row_count, HALF), lambda p, at, who, h=h: (0, at[2 * p + h])) for h in (0, 1)
    ]
    operands = [cols, cols]
    for image in images:
        for h in (0, 1):
            specs.append(
                pl.BlockSpec(
                    (3, image.shape[1], HALF), lambda p, at, who, h=h: (0, 0, at[2 * p + h])
                )
            )
            operands.append(image)
    specs.append(pl.BlockSpec(gathered.shape, lambda p, at, who: (0, 0, 0)))
    operands.append(gathered)
    return pl.pallas_call(
        functools.partial(rotate_kernel, pair_count),
        out_shape=(
            jax.ShapeDtypeStruct((row_count, orb_count), BF16),
            jax.ShapeDtypeStruct((3, row_count, orb_count), BF16),
            jax.ShapeDtypeStruct((3, orb_count // HALF, HALF), F32),
        ),
        grid_spec=pltpu.PrefetchScalarGridSpec(
            num_scalar_prefetch=2,
            grid=(pair_count,),
            in_specs=specs,
            out_specs=(
                pl.BlockSpec((row_count, PAIR), lambda p, at, who: (0, p)),
                pl.BlockSpec((3, row_count, PAIR), lambda p, at, who: (0, 0, p)),
                pl.BlockSpec((3, orb_count // HALF, HALF), lambda p, at, who: (0, 0, 0)),
            ),
        ),
        compiler_params=params(),
        name="rotate",
    )(place, me, *operands)


def last_kernel(
    pair_count, place_ref, home_ref, me_ref, first_ref, second_ref, gathered_ref, out_ref, held_ref
):
    p, h = pl.program_id(0), pl.program_id(1)

    @pl.when(h == 0)
    def _():
        rotation = assemble(gathered_ref, me_ref[0], pair_count, p)
        cols = jnp.concatenate([first_ref[...], second_ref[...]], axis=1)
        turned = jnp.dot(cols, rotation, preferred_element_type=F32).astype(BF16)
        out_ref[...] = turned[:, :HALF]
        held_ref[...] = turned[:, HALF:]

    @pl.when(h == 1)
    def _():
        out_ref[...] = held_ref[...]


def rotate_last(place, home, me, cols, gathered):
    row_count, orb_count = cols.shape
    pair_count = orb_count // PAIR
    return pl.pallas_call(
        functools.partial(last_kernel, pair_count),
        out_shape=jax.ShapeDtypeStruct((row_count, orb_count), BF16),
        grid_spec=pltpu.PrefetchScalarGridSpec(
            num_scalar_prefetch=3,
            grid=(pair_count, 2),
            in_specs=[
                pl.BlockSpec((row_count, HALF), lambda p, h, at, to, who: (0, at[2 * p])),
                pl.BlockSpec((row_count, HALF), lambda p, h, at, to, who: (0, at[2 * p + 1])),
                pl.BlockSpec(gathered.shape, lambda p, h, at, to, who: (0, 0, 0)),
            ],
            out_specs=pl.BlockSpec((row_count, HALF), lambda p, h, at, to, who: (0, to[2 * p + h])),
            scratch_shapes=[pltpu.VMEM((row_count, HALF), BF16)],
        ),
        compiler_params=params(),
        name="rotate_last",
    )(place, home, me, cols, cols, gathered)


def sum_all(value):
    count = lax.axis_size("orb")
    for bit in range(bits_of(count)):
        value = value + swap(value, 1 << bit)
    return value


def spread(value, bits, me, low_bit):
    ways = 1 << bits
    mine = (me >> low_bit) & (ways - 1)
    value = value.reshape((ways, -1) + value.shape[1:])
    pieces = [
        swap(
            lax.dynamic_index_in_dim(value, mine ^ q, 0, keepdims=False).astype(WIRE), q << low_bit
        )
        for q in range(1, ways)
    ]
    own = lax.dynamic_index_in_dim(value, mine, 0, keepdims=False)
    for piece in pieces:
        own = own + piece.astype(F32)
    return own


def reduce_pairs(keep, send, me):
    pair_count = keep.shape[0]
    pair_bits = bits_of(pair_count)
    sub_bits = bits_of(lax.axis_size("orb")) - pair_bits
    value = keep + swap(send, 1)
    for bit in range(1, sub_bits):
        rows = value.shape[1] // 2
        value = jnp.swapaxes(value.reshape(pair_count, 2, rows, HALF), 0, 1)
        value = spread(value.reshape(2 * pair_count, rows, HALF), 1, me, bit)
    high = pair_count // 2
    rows = value.shape[1]
    value = jnp.swapaxes(value.reshape(high, 2, rows, HALF), 0, 1).reshape(pair_count, rows, HALF)
    value = spread(value, 1, me, sub_bits)
    value = spread(value, pair_bits - 1, me, sub_bits + 1)
    return value[0]


def gather_bits(value, bits, low_bit):
    return jnp.concatenate(
        [value] + [swap(value, q << low_bit) for q in range(1, 1 << bits)], axis=0
    )


def per_device(orbitals, dipole_blocks, coupling_mask, matchings):
    row_count, orb_count = orbitals.shape
    count = lax.axis_size("orb")
    block_count = orb_count // HALF
    pair_count = orb_count // PAIR
    pair_bits = bits_of(pair_count)
    sub_bits = bits_of(count) - pair_bits
    basis_count = row_count * count
    block_rows = row_count // BLK
    position = lax.axis_index("orb").astype(jnp.int32)
    me = position.reshape(1)

    forward = [(i, i + 1) for i in range(count - 1)]
    backward = [(i + 1, i) for i in range(count - 1)]
    low = lax.ppermute(orbitals[row_count - BLK :], "orb", forward)
    high = lax.ppermute(orbitals[:BLK], "orb", backward)
    mask_full = jnp.stack(
        [coupling_mask[:, 0], jnp.ones((block_rows,), jnp.int32), coupling_mask[:, 1]], axis=1
    ).astype(BF16)
    blocks = jnp.transpose(
        dipole_blocks * mask_full[None, :, :, None, None], (1, 0, 3, 2, 4)
    ).reshape(block_rows, 3 * BLK, 3 * BLK)
    inner, diag = inner_images(blocks, orbitals)
    edge, diag = edge_images(blocks, orbitals, low, high, diag)

    cols, images = orbitals, (inner, edge)
    ident = jnp.arange(block_count, dtype=jnp.int32)
    held = ident
    for round_index in range(ROUNDS):
        matching = matchings[round_index].astype(jnp.int32)
        found = jnp.where(matching[:, None] == held[None, :], ident[None, :], 0)
        place = jnp.sum(found, axis=1).astype(jnp.int32)
        diag_sum = sum_all(diag)
        sums = pair_sums(place, cols, images)
        keep, send = weigh(place, me, sums, diag_sum)
        own = reduce_pairs(keep, send, position)
        packed = own[None]
        for bit in range(sub_bits):
            packed = gather_bits(packed, 1, bit)
        share = rotation_share(0.01 / basis_count, me, packed)
        gathered = gather_bits(share[None], 1, sub_bits)
        gathered = gather_bits(gathered, pair_bits - 1, sub_bits + 1)
        for bit in range(sub_bits):
            gathered = gather_bits(gathered, 1, bit)
        if round_index + 1 < ROUNDS:
            cols, moved, diag = rotate(place, me, cols, images, gathered)
            images = (moved,)
            held = matching
    return rotate_last(place, matching, me, cols, gathered)


def solution(mesh):
    in_specs = (
        P("orb", "groups"),
        P("groups", "orb", None, None, None),
        P("orb", "groups"),
        P("groups", None),
    )
    out_specs = P("orb", "groups")
    return jax.shard_map(
        per_device, mesh=mesh, in_specs=in_specs, out_specs=out_specs, check_vma=False
    )
```

```python
import functools

import jax
import jax.numpy as jnp
from jax import lax
from jax.experimental import pallas as pl
from jax.experimental.pallas import tpu as pltpu
from jax.sharding import PartitionSpec as P

HALF = 128
BLK = 128
ROUNDS = 2
PAIR = 2 * HALF
F32 = jnp.float32
BF16 = jnp.bfloat16
VMEM_LIMIT = 24 * 1024 * 1024
VMEM = pl.BlockSpec(memory_space=pltpu.VMEM)
SMEM = pl.BlockSpec(memory_space=pltpu.SMEM)
TILE = 512
SMALL = 3e-8
WIRE = BF16


def params():
    return pltpu.CompilerParams(vmem_limit_bytes=VMEM_LIMIT)


def bits_of(count):
    return count.bit_length() - 1


def bitrev(value, bits):
    return sum(((value >> j) & 1) << (bits - 1 - j) for j in range(bits))


def swap(block, distance):
    count = lax.axis_size("orb")
    return lax.ppermute(block, "orb", [(i, i ^ distance) for i in range(count)])


def put_diag(diag_ref, component, block, cols, image, first):
    total = jnp.sum(cols.astype(F32) * image.astype(F32), axis=0, keepdims=True)
    for half in range(total.shape[1] // HALF):
        spot = pl.ds(block + half, 1)
        piece = total[:, half * HALF : (half + 1) * HALF]
        if first:
            diag_ref[component, spot, :] = piece
        else:
            diag_ref[component, spot, :] += piece


def edge_rows_kernel(last_ref, first_ref, last_out_ref, first_out_ref):
    last_out_ref[...] = last_ref[...]
    first_out_ref[...] = first_ref[...]


def edge_rows(orbitals):
    row_count, orb_count = orbitals.shape
    shape = jax.ShapeDtypeStruct((BLK, orb_count), BF16)
    return pl.pallas_call(
        edge_rows_kernel,
        out_shape=(shape, shape),
        grid=(1,),
        in_specs=[
            pl.BlockSpec((BLK, orb_count), lambda i: (row_count // BLK - 1, 0)),
            pl.BlockSpec((BLK, orb_count), lambda i: (0, 0)),
        ],
        out_specs=(VMEM, VMEM),
        compiler_params=params(),
        name="edge_rows",
    )(orbitals, orbitals)


def inner_kernel(block_rows, blocks_ref, cols_ref, image_ref, diag_ref):
    for start in range(0, cols_ref.shape[1], TILE):
        tile = slice(start, start + TILE)
        for b in range(1, block_rows - 1):
            out = jnp.dot(
                blocks_ref[b],
                cols_ref[(b - 1) * BLK : (b + 2) * BLK, tile],
                preferred_element_type=F32,
            ).astype(BF16)
            own = cols_ref[b * BLK : (b + 1) * BLK, tile]
            for k in range(3):
                image = out[k * BLK : (k + 1) * BLK]
                image_ref[k, (b - 1) * BLK : b * BLK, tile] = image
                put_diag(diag_ref, k, start // HALF, own, image, b == 1)


def inner_images(blocks, orbitals):
    row_count, orb_count = orbitals.shape
    block_rows = row_count // BLK
    return pl.pallas_call(
        functools.partial(inner_kernel, block_rows),
        out_shape=(
            jax.ShapeDtypeStruct((3, row_count - 2 * BLK, orb_count), BF16),
            jax.ShapeDtypeStruct((3, orb_count // HALF, HALF), F32),
        ),
        in_specs=[VMEM, VMEM],
        out_specs=(VMEM, VMEM),
        compiler_params=params(),
        name="inner_images",
    )(blocks, orbitals)


def edge_kernel(block_rows, blocks_ref, cols_ref, low_ref, high_ref, start_ref, image_ref, diag_ref):
    diag_ref[...] = start_ref[...]
    for start in range(0, cols_ref.shape[1], TILE):
        tile = slice(start, start + TILE)
        for place, b in ((0, 0), (1, block_rows - 1)):
            if b == 0:
                window = jnp.concatenate([low_ref[:, tile], cols_ref[: 2 * BLK, tile]], axis=0)
            else:
                window = jnp.concatenate(
                    [cols_ref[(b - 1) * BLK :, tile], high_ref[:, tile]], axis=0
                )
            out = jnp.dot(blocks_ref[b], window, preferred_element_type=F32).astype(BF16)
            own = cols_ref[b * BLK : (b + 1) * BLK, tile]
            for k in range(3):
                image = out[k * BLK : (k + 1) * BLK]
                image_ref[k, place * BLK : (place + 1) * BLK, tile] = image
                put_diag(diag_ref, k, start // HALF, own, image, False)


def edge_images(blocks, orbitals, low, high, start):
    row_count, orb_count = orbitals.shape
    block_rows = row_count // BLK
    return pl.pallas_call(
        functools.partial(edge_kernel, block_rows),
        out_shape=(
            jax.ShapeDtypeStruct((3, 2 * BLK, orb_count), BF16),
            jax.ShapeDtypeStruct((3, orb_count // HALF, HALF), F32),
        ),
        in_specs=[VMEM] * 5,
        out_specs=(VMEM, VMEM),
        compiler_params=params(),
        name="edge_images",
    )(blocks, orbitals, low, high, start)


def lower_mask():
    rows = lax.broadcasted_iota(jnp.int32, (HALF, HALF), 0)
    cols = lax.broadcasted_iota(jnp.int32, (HALF, HALF), 1)
    return rows > cols


def pair_columns(ref, lead, places):
    return jnp.concatenate(
        [ref[lead + (slice(None), pl.ds(pl.multiple_of(at * HALF, HALF), HALF))] for at in places],
        axis=1,
    )


def pair_image(refs, component, places):
    pieces = [pair_columns(ref, (component,), places) for ref in refs]
    if len(pieces) == 1:
        return pieces[0]
    inner, edge = pieces
    return jnp.concatenate([edge[:BLK], inner, edge[BLK:]], axis=0)


def gram_kernel(first, place_ref, cols_ref, *refs):
    image_refs, mats_ref = refs[:-1], refs[-1]
    for i in range(mats_ref.shape[0]):
        places = [place_ref[2 * (first + i) + h] for h in (0, 1)]
        cols = pair_columns(cols_ref, (), places)
        images = jnp.concatenate([pair_image(image_refs, k, places) for k in range(3)], axis=1)
        mats_ref[i] = lax.dot_general(
            cols, images, (((0,), (0,)), ((), ())), preferred_element_type=F32
        )


def pair_products(place, cols, images, first, count):
    return pl.pallas_call(
        functools.partial(gram_kernel, first),
        out_shape=jax.ShapeDtypeStruct((count, PAIR, 3 * PAIR), F32),
        in_specs=[SMEM] + [VMEM] * (1 + len(images)),
        out_specs=VMEM,
        compiler_params=params(),
        name="pair_products",
    )(place, cols, *images)


def weight_kernel(first, place_ref, me_ref, diag_ref, *refs):
    mats_refs, keep_ref, send_ref = refs[:-2], refs[-2], refs[-1]
    mine = (me_ref[0] & 1) == 0
    low = lower_mask()
    p = 0
    for mats_ref in mats_refs:
        for i in range(mats_ref.shape[0]):
            halves = [
                [diag_ref[k, pl.ds(place_ref[2 * (first + p) + h], 1), :] for k in range(3)] for h in (0, 1)
            ]
            turned = jnp.concatenate(
                [jnp.concatenate(half + half + half[:2], axis=0).T for half in halves], axis=0
            )
            total = jnp.zeros((PAIR, PAIR), F32)
            for k in range(3):
                row = jnp.concatenate([half[k] for half in halves], axis=1)
                total += mats_ref[i, :, k * PAIR : (k + 1) * PAIR] * (turned[:, k : k + 1] - row)
            one, two = total[:HALF, :HALF], total[HALF:, HALF:]
            cross = total[:HALF, HALF:] - total[HALF:, :HALF].T
            within = jnp.where(low, one, two) - jnp.where(low, two, one).T
            keep_ref[p] = jnp.where(mine, cross, within)
            send_ref[p] = jnp.where(mine, within, cross)
            p += 1


def weigh(place, me, diag, mats, first):
    pair_count = sum(mat.shape[0] for mat in mats)
    shape = jax.ShapeDtypeStruct((pair_count, HALF, HALF), F32)
    return pl.pallas_call(
        functools.partial(weight_kernel, first),
        out_shape=(shape, shape),
        in_specs=[SMEM, SMEM] + [VMEM] * (1 + len(mats)),
        out_specs=(VMEM, VMEM),
        compiler_params=params(),
        name="weigh",
    )(place, me, diag, *mats)


def matmul(left, right):
    return jnp.dot(left, right, precision=lax.Precision.HIGHEST, preferred_element_type=F32)


def rotation_kernel(scale, subs, me_ref, packed_ref, out_ref, sum_ref, power_ref):
    sub = me_ref[0] & (subs - 1)
    pieces = [packed_ref[bitrev(i, bits_of(subs)) ^ sub] for i in range(subs)]
    packed = jnp.concatenate(pieces, axis=0) * scale
    cross, within = packed[:HALF], packed[HALF:]
    low = lower_mask()
    first = jnp.where(low, within, 0.0)
    second = jnp.where(low, 0.0, within)
    half_gen = jnp.concatenate(
        [
            jnp.concatenate([first - first.T, cross], axis=1),
            jnp.concatenate([-cross.T, second - second.T], axis=1),
        ],
        axis=0,
    )
    rows = lax.broadcasted_iota(jnp.int32, (PAIR, PAIR), 0)
    cols = lax.broadcasted_iota(jnp.int32, (PAIR, PAIR), 1)
    eye = jnp.where(rows == cols, 1.0, 0.0).astype(F32)
    square = -matmul(half_gen, half_gen)
    fourth = matmul(square, square)
    bound = 1.0001 * jnp.sqrt(jnp.max(jnp.sum(jnp.abs(fourth), axis=1)))
    factor = 2.0 / (2.0 + bound)
    rest = 1.0 - factor
    sum_ref[...] = factor * ((1.0 + rest) * eye - factor * square)
    power_ref[...] = rest * rest * eye - (2.0 * rest * factor) * square + factor * factor * fourth

    def going(state):
        step, left = state
        return jnp.logical_and(step < 24, left > SMALL)

    def body(state):
        step, left = state
        power = power_ref[...]
        sum_ref[...] += matmul(sum_ref[...], power)

        @pl.when(left * left > SMALL)
        def _():
            power_ref[...] = matmul(power, power)

        return step + 1, left * left

    reach = bound / (2.0 + bound)
    lax.while_loop(going, body, (jnp.int32(0), reach * reach))
    result = 2.0 * matmul(eye + half_gen, sum_ref[...]) - eye
    share = PAIR // subs
    for i in range(subs):

        @pl.when(sub == i)
        def _():
            out_ref[...] = result[i * share : (i + 1) * share].astype(BF16)


def rotation_share(scale, me, packed):
    subs = packed.shape[0]
    return pl.pallas_call(
        functools.partial(rotation_kernel, scale, subs),
        out_shape=jax.ShapeDtypeStruct((PAIR // subs, PAIR), BF16),
        in_specs=[SMEM, VMEM],
        out_specs=VMEM,
        scratch_shapes=[pltpu.VMEM((PAIR, PAIR), F32), pltpu.VMEM((PAIR, PAIR), F32)],
        compiler_params=params(),
        name="rotation",
    )(me, packed)


def assemble(gathered_ref, me, pair_count, pair):
    subs = PAIR // gathered_ref.shape[1]
    my_sub, my_pair = me & (subs - 1), me // subs
    return jnp.concatenate(
        [gathered_ref[(i ^ my_sub) * pair_count + (pair ^ my_pair)] for i in range(subs)], axis=0
    )


def rotate_kernel(pair_count, place_ref, me_ref, gathered_ref, cols_ref, *refs):
    image_refs, (out_ref, image_ref, diag_ref) = refs[:-3], refs[-3:]
    for p in range(pair_count):
        rotation = assemble(gathered_ref, me_ref[0], pair_count, p)
        places = [place_ref[2 * p + h] for h in (0, 1)]
        spot = slice(p * PAIR, (p + 1) * PAIR)
        cols = pair_columns(cols_ref, (), places)
        turned = jnp.dot(cols, rotation, preferred_element_type=F32).astype(BF16)
        out_ref[:, spot] = turned
        for k in range(3):
            image = pair_image(image_refs, k, places)
            moved = jnp.dot(image, rotation, preferred_element_type=F32).astype(BF16)
            image_ref[k, :, spot] = moved
            put_diag(diag_ref, k, 2 * p, turned, moved, True)


def rotate(place, me, gathered, cols, images):
    row_count, orb_count = cols.shape
    return pl.pallas_call(
        functools.partial(rotate_kernel, orb_count // PAIR),
        out_shape=(
            jax.ShapeDtypeStruct((row_count, orb_count), BF16),
            jax.ShapeDtypeStruct((3, row_count, orb_count), BF16),
            jax.ShapeDtypeStruct((3, orb_count // HALF, HALF), F32),
        ),
        in_specs=[SMEM, SMEM] + [VMEM] * (2 + len(images)),
        out_specs=(VMEM, VMEM, VMEM),
        compiler_params=params(),
        name="rotate",
    )(place, me, gathered, cols, *images)


def last_kernel(pair_count, place_ref, home_ref, me_ref, gathered_ref, cols_ref, out_ref):
    for p in range(pair_count):
        rotation = assemble(gathered_ref, me_ref[0], pair_count, p)
        places = [place_ref[2 * p + h] for h in (0, 1)]
        cols = pair_columns(cols_ref, (), places)
        turned = jnp.dot(cols, rotation, preferred_element_type=F32).astype(BF16)
        for h in (0, 1):
            home = pl.multiple_of(home_ref[2 * p + h] * HALF, HALF)
            out_ref[:, pl.ds(home, HALF)] = turned[:, h * HALF : (h + 1) * HALF]


def rotate_last(place, home, me, gathered, cols):
    row_count, orb_count = cols.shape
    rows = row_count // 2
    return pl.pallas_call(
        functools.partial(last_kernel, orb_count // PAIR),
        out_shape=jax.ShapeDtypeStruct((row_count, orb_count), BF16),
        grid=(row_count // rows,),
        in_specs=[
            SMEM,
            SMEM,
            SMEM,
            pl.BlockSpec(gathered.shape, lambda r: (0, 0, 0)),
            pl.BlockSpec((rows, orb_count), lambda r: (r, 0)),
        ],
        out_specs=pl.BlockSpec((rows, orb_count), lambda r: (r, 0)),
        compiler_params=params(),
        name="rotate_last",
    )(place, home, me, gathered, cols)


def sum_beside(diag, makers):
    made = []
    hops = bits_of(lax.axis_size("orb"))
    for bit in range(hops):
        arrived = swap(diag, 1 << bit)
        if bit < len(makers):
            diag, arrived, product = lax.optimization_barrier((diag, arrived, makers[bit](diag)))
            made.append(product)
        diag = diag + arrived
    return diag, made


def places_of(position, sub_bits, pair_bits):
    steps = [(bit, 1) for bit in range(1, sub_bits)] + [(sub_bits, 1), (sub_bits + 1, pair_bits - 1)]
    found = {}
    for low_bit, bits in steps:
        mine = (position >> low_bit) & ((1 << bits) - 1)
        found[low_bit] = [(mine ^ q).astype(jnp.uint32) for q in range(1 << bits)]
    return found


def pick(value, at):
    zero = jnp.uint32(0)
    start = (at,) + (zero,) * (value.ndim - 1)
    return lax.dynamic_slice(value, start, (1,) + value.shape[1:])[0]


def spread(value, places, low_bit, wire):
    ways = len(places)
    value = value.reshape((ways, -1) + value.shape[1:])
    pieces = [swap(pick(value, places[q]).astype(wire), q << low_bit) for q in range(1, ways)]
    own = pick(value, places[0])
    for piece in pieces:
        own = own + piece.astype(F32)
    return own


def reduce_pairs(value, places, sub_bits):
    pair_count = value.shape[0]
    for bit in range(1, sub_bits):
        rows = value.shape[1] // 2
        value = jnp.swapaxes(value.reshape(pair_count, 2, rows, HALF), 0, 1)
        value = spread(value.reshape(2 * pair_count, rows, HALF), places[bit], bit, F32)
    rows = value.shape[1]
    value = value.reshape(pair_count // 2, 2, rows, HALF)
    value = jnp.swapaxes(value, 0, 1).reshape(pair_count, rows, HALF)
    value = spread(value, places[sub_bits], sub_bits, BF16)
    return spread(value, places[sub_bits + 1], sub_bits + 1, WIRE)[0]


def gather_bits(value, bits, low_bit):
    return jnp.concatenate(
        [value] + [swap(value, q << low_bit) for q in range(1, 1 << bits)], axis=0
    )


def per_device(orbitals, dipole_blocks, coupling_mask, matchings):
    row_count, orb_count = orbitals.shape
    count = lax.axis_size("orb")
    block_count = orb_count // HALF
    pair_count = orb_count // PAIR
    pair_bits = bits_of(pair_count)
    sub_bits = bits_of(count) - pair_bits
    basis_count = row_count * count
    block_rows = row_count // BLK
    position = lax.axis_index("orb").astype(jnp.int32)
    places = places_of(position, sub_bits, pair_bits)
    ident = jnp.arange(block_count, dtype=jnp.int32)
    held = [ident] + [matchings[r] for r in range(ROUNDS - 1)]
    spots = []
    for r in range(ROUNDS):
        found = jnp.where(matchings[r][:, None] == held[r][None, :], ident[None, :], 0)
        spots.append(jnp.sum(found, axis=1).astype(jnp.int32))
    orbitals, places, spots, me = lax.optimization_barrier(
        (orbitals, places, spots, position.reshape(1))
    )

    forward = [(i, i + 1) for i in range(count - 1)]
    backward = [(i + 1, i) for i in range(count - 1)]
    last, first = edge_rows(orbitals)
    low = lax.ppermute(last, "orb", forward)
    high = lax.ppermute(first, "orb", backward)
    mask_full = jnp.stack(
        [coupling_mask[:, 0], jnp.ones((block_rows,), jnp.int32), coupling_mask[:, 1]], axis=1
    ).astype(BF16)
    blocks = jnp.transpose(
        dipole_blocks * mask_full[None, :, :, None, None], (1, 0, 3, 2, 4)
    ).reshape(block_rows, 3 * BLK, 3 * BLK)
    inner, diag = inner_images(blocks, orbitals)
    edge, diag = edge_images(blocks, orbitals, low, high, diag)

    cols, images = orbitals, (inner, edge)
    for round_index in range(ROUNDS):
        place = spots[round_index]
        splits = 4
        step = pair_count // splits

        def product(start, token):
            held_cols, _ = lax.optimization_barrier((cols, token))
            return pair_products(place, held_cols, images, start, step)

        makers = [functools.partial(product, i * step) for i in range(splits)]
        diag_sum, mats = sum_beside(diag, makers)
        half = splits // 2
        keep_a, send_a = weigh(place, me, diag_sum, mats[:half], 0)
        came_a = swap(send_a, 1)
        keep_b, send_b = weigh(place, me, diag_sum, mats[half:], half * step)
        came_a, keep_b, send_b = lax.optimization_barrier((came_a, keep_b, send_b))
        value = jnp.concatenate([keep_a + came_a, keep_b + swap(send_b, 1)], axis=0)
        own = reduce_pairs(value, places, sub_bits)
        packed = own[None]
        for bit in range(sub_bits):
            packed = gather_bits(packed, 1, bit)
        share = rotation_share(0.01 / basis_count, me, packed)
        gathered = gather_bits(share[None], 1, sub_bits)
        gathered = gather_bits(gathered, pair_bits - 1, sub_bits + 1)
        for bit in range(sub_bits):
            gathered = gather_bits(gathered, 1, bit)
        if round_index + 1 < ROUNDS:
            cols, moved, diag = rotate(place, me, gathered, cols, images)
            images = (moved,)
    return rotate_last(place, matchings[ROUNDS - 1], me, gathered, cols)


def solution(mesh):
    in_specs = (
        P("orb", "groups"),
        P("groups", "orb", None, None, None),
        P("orb", "groups"),
        P("groups", None),
    )
    out_specs = P("orb", "groups")
    return jax.shard_map(
        per_device, mesh=mesh, in_specs=in_specs, out_specs=out_specs, check_vma=False
    )
```

```python
import functools

import jax
import jax.numpy as jnp
from jax import lax
from jax.experimental import pallas as pl
from jax.experimental.pallas import tpu as pltpu
from jax.sharding import PartitionSpec as P

HALF = 128
BLK = 128
ROUNDS = 2
PAIR = 2 * HALF
F32 = jnp.float32
BF16 = jnp.bfloat16
VMEM_LIMIT = 24 * 1024 * 1024
VMEM = pl.BlockSpec(memory_space=pltpu.VMEM)
SMEM = pl.BlockSpec(memory_space=pltpu.SMEM)
TILE = 512
SMALL = 1e-6
WIRE = BF16


def params(limit=VMEM_LIMIT):
    return pltpu.CompilerParams(vmem_limit_bytes=limit)


def bits_of(count):
    return count.bit_length() - 1


def bitrev(value, bits):
    return sum(((value >> j) & 1) << (bits - 1 - j) for j in range(bits))


def swap(block, distance):
    count = lax.axis_size("orb")
    return lax.ppermute(block, "orb", [(i, i ^ distance) for i in range(count)])


def put_diag(diag_ref, component, block, cols, image, first):
    total = jnp.sum(cols.astype(F32) * image.astype(F32), axis=0, keepdims=True)
    for half in range(total.shape[1] // HALF):
        spot = pl.ds(block + half, 1)
        piece = total[:, half * HALF : (half + 1) * HALF]
        if first:
            diag_ref[component, spot, :] = piece
        else:
            diag_ref[component, spot, :] += piece


def edge_rows_kernel(orbitals_ref, last_ref, first_ref, held_ref, sems):
    row_count = orbitals_ref.shape[0]
    spots = (orbitals_ref.at[row_count - BLK :], orbitals_ref.at[:BLK])
    loads = [pltpu.make_async_copy(spots[i], held_ref.at[i], sems.at[i]) for i in (0, 1)]
    stores = [
        pltpu.make_async_copy(held_ref.at[i], (last_ref, first_ref)[i], sems.at[2 + i])
        for i in (0, 1)
    ]
    for load in loads:
        load.start()
    for load, store in zip(loads, stores):
        load.wait()
        store.start()
    for store in stores:
        store.wait()


def edge_rows(orbitals):
    shape = jax.ShapeDtypeStruct((BLK, orbitals.shape[1]), BF16)
    hbm = pl.BlockSpec(memory_space=pltpu.HBM)
    return pl.pallas_call(
        edge_rows_kernel,
        out_shape=(shape, shape),
        in_specs=[hbm],
        out_specs=(hbm, hbm),
        scratch_shapes=[
            pltpu.VMEM((2, BLK, orbitals.shape[1]), BF16),
            pltpu.SemaphoreType.DMA((4,)),
        ],
        compiler_params=params(56 * 1024 * 1024),
        name="edge_rows",
    )(orbitals)


def inner_kernel(block_rows, blocks_ref, cols_ref, image_ref, diag_ref):
    for start in range(0, cols_ref.shape[1], TILE):
        tile = slice(start, start + TILE)
        for b in range(1, block_rows - 1):
            out = jnp.dot(
                blocks_ref[b],
                cols_ref[(b - 1) * BLK : (b + 2) * BLK, tile],
                preferred_element_type=F32,
            ).astype(BF16)
            own = cols_ref[b * BLK : (b + 1) * BLK, tile]
            for k in range(3):
                image = out[k * BLK : (k + 1) * BLK]
                image_ref[k, (b - 1) * BLK : b * BLK, tile] = image
                put_diag(diag_ref, k, start // HALF, own, image, b == 1)


def inner_images(blocks, orbitals):
    row_count, orb_count = orbitals.shape
    block_rows = row_count // BLK
    return pl.pallas_call(
        functools.partial(inner_kernel, block_rows),
        out_shape=(
            jax.ShapeDtypeStruct((3, row_count - 2 * BLK, orb_count), BF16),
            jax.ShapeDtypeStruct((3, orb_count // HALF, HALF), F32),
        ),
        in_specs=[VMEM, VMEM],
        out_specs=(VMEM, VMEM),
        compiler_params=params(),
        name="inner_images",
    )(blocks, orbitals)


def edge_kernel(block_rows, blocks_ref, cols_ref, low_ref, high_ref, start_ref, image_ref, diag_ref):
    diag_ref[...] = start_ref[...]
    for start in range(0, cols_ref.shape[1], TILE):
        tile = slice(start, start + TILE)
        for place, b in ((0, 0), (1, block_rows - 1)):
            if b == 0:
                window = jnp.concatenate([low_ref[:, tile], cols_ref[: 2 * BLK, tile]], axis=0)
            else:
                window = jnp.concatenate(
                    [cols_ref[(b - 1) * BLK :, tile], high_ref[:, tile]], axis=0
                )
            out = jnp.dot(blocks_ref[b], window, preferred_element_type=F32).astype(BF16)
            own = cols_ref[b * BLK : (b + 1) * BLK, tile]
            for k in range(3):
                image = out[k * BLK : (k + 1) * BLK]
                image_ref[k, place * BLK : (place + 1) * BLK, tile] = image
                put_diag(diag_ref, k, start // HALF, own, image, False)


def edge_images(blocks, orbitals, low, high, start):
    row_count, orb_count = orbitals.shape
    block_rows = row_count // BLK
    return pl.pallas_call(
        functools.partial(edge_kernel, block_rows),
        out_shape=(
            jax.ShapeDtypeStruct((3, 2 * BLK, orb_count), BF16),
            jax.ShapeDtypeStruct((3, orb_count // HALF, HALF), F32),
        ),
        in_specs=[VMEM] * 5,
        out_specs=(VMEM, VMEM),
        compiler_params=params(),
        name="edge_images",
    )(blocks, orbitals, low, high, start)


def lower_mask():
    rows = lax.broadcasted_iota(jnp.int32, (HALF, HALF), 0)
    cols = lax.broadcasted_iota(jnp.int32, (HALF, HALF), 1)
    return rows > cols


def pair_columns(ref, lead, places):
    return jnp.concatenate(
        [ref[lead + (slice(None), pl.ds(pl.multiple_of(at * HALF, HALF), HALF))] for at in places],
        axis=1,
    )


def pair_image(refs, component, places):
    pieces = [pair_columns(ref, (component,), places) for ref in refs]
    if len(pieces) == 1:
        return pieces[0]
    inner, edge = pieces
    return jnp.concatenate([edge[:BLK], inner, edge[BLK:]], axis=0)


def gram_kernel(first, place_ref, me_ref, cols_ref, *refs):
    image_refs, keep_ref, send_ref = refs[:-2], refs[-2], refs[-1]
    mine = (me_ref[0] & 1) == 0
    low = lower_mask()
    for i in range(keep_ref.shape[0]):
        places = [place_ref[2 * (first + i) + h] for h in (0, 1)]
        cols = pair_columns(cols_ref, (), places)
        images = jnp.concatenate([pair_image(image_refs, k, places) for k in range(3)], axis=1)
        mats = lax.dot_general(cols, images, (((0,), (0,)), ((), ())), preferred_element_type=F32)
        for k in range(3):
            mat = mats[:, k * PAIR : (k + 1) * PAIR]
            one, two = mat[:HALF, :HALF], mat[HALF:, HALF:]
            cross = mat[:HALF, HALF:] + mat[HALF:, :HALF].T
            within = jnp.where(low, one, two) + jnp.where(low, two, one).T
            keep_ref[i, k] = jnp.where(mine, cross, within)
            send_ref[i, k] = jnp.where(mine, within, cross)


def pair_products(place, me, cols, images, first, count):
    shape = jax.ShapeDtypeStruct((count, 3, HALF, HALF), F32)
    return pl.pallas_call(
        functools.partial(gram_kernel, first),
        out_shape=(shape, shape),
        in_specs=[SMEM, SMEM] + [VMEM] * (1 + len(images)),
        out_specs=(VMEM, VMEM),
        compiler_params=params(),
        name="pair_products",
    )(place, me, cols, *images)


def weight_kernel(sub_bits, place_ref, me_ref, diag_ref, *refs):
    sums_refs, keep_ref, send_ref = refs[:-2], refs[-2], refs[-1]
    kept_refs, came_refs = sums_refs[: len(sums_refs) // 2], sums_refs[len(sums_refs) // 2 :]
    core = me_ref[0] & 1
    bit = (me_ref[0] >> sub_bits) & 1
    rows = lax.broadcasted_iota(jnp.int32, (HALF, HALF), 0)
    cols = lax.broadcasted_iota(jnp.int32, (HALF, HALF), 1)
    low = jnp.where(rows > cols, 1, 0)
    col_first = jnp.maximum(low, 1 - core) > 0
    row_first = jnp.minimum(low, core) > 0
    step = kept_refs[0].shape[0]
    for j in range(keep_ref.shape[0]):
        for stays in (True, False):
            odd = bit if stays else 1 - bit
            pair = 2 * j + odd
            i = 2 * j % step + odd
            kept_ref, came_ref = kept_refs[2 * j // step], came_refs[2 * j // step]
            halves = [
                [diag_ref[k, pl.ds(place_ref[2 * pair + h], 1), :] for k in range(3)]
                for h in (0, 1)
            ]
            first, second = [
                jnp.concatenate(half + half + half[:2], axis=0).T for half in halves
            ]
            total = jnp.zeros((HALF, HALF), F32)
            for k in range(3):
                col = jnp.where(col_first, first[:, k : k + 1], second[:, k : k + 1])
                row = jnp.where(row_first, halves[0][k], halves[1][k])
                total += (kept_ref[i, k] + came_ref[i, k]) * (col - row)
            if stays:
                keep_ref[j] = total
            else:
                send_ref[j] = total.astype(BF16)


def weigh(place, me, diag, kept, came, sub_bits):
    high = sum(part.shape[0] for part in kept) // 2
    return pl.pallas_call(
        functools.partial(weight_kernel, sub_bits),
        out_shape=(
            jax.ShapeDtypeStruct((high, HALF, HALF), F32),
            jax.ShapeDtypeStruct((high, HALF, HALF), BF16),
        ),
        in_specs=[SMEM, SMEM] + [VMEM] * (1 + 2 * len(kept)),
        out_specs=(VMEM, VMEM),
        compiler_params=params(),
        name="weigh",
    )(place, me, diag, *kept, *came)


def matmul(left, right):
    return jnp.dot(left, right, precision=lax.Precision.HIGHEST, preferred_element_type=F32)


def parts_of(value):
    high = value.astype(BF16)
    return high, (value - high.astype(F32)).astype(BF16)


def by_parts(left, right):
    left_high, left_low = parts_of(left)
    right_high, right_low = parts_of(right)
    rows = left.shape[0]
    both = jnp.dot(
        jnp.concatenate([left_high, left_low], axis=0), right_high, preferred_element_type=F32
    )
    return both[:rows] + (
        both[rows:] + jnp.dot(left_high, right_low, preferred_element_type=F32)
    )


def rotation_kernel(scale, subs, me_ref, packed_ref, out_ref, sum_ref, power_ref):
    sub = me_ref[0] & (subs - 1)
    pieces = [packed_ref[bitrev(i, bits_of(subs)) ^ sub] for i in range(subs)]
    packed = jnp.concatenate(pieces, axis=0) * scale
    cross, within = packed[:HALF], packed[HALF:]
    low = lower_mask()
    first = jnp.where(low, within, 0.0)
    second = jnp.where(low, 0.0, within)
    half_gen = jnp.concatenate(
        [
            jnp.concatenate([first - first.T, cross], axis=1),
            jnp.concatenate([-cross.T, second - second.T], axis=1),
        ],
        axis=0,
    )
    rows = lax.broadcasted_iota(jnp.int32, (PAIR, PAIR), 0)
    cols = lax.broadcasted_iota(jnp.int32, (PAIR, PAIR), 1)
    eye = jnp.where(rows == cols, 1.0, 0.0).astype(F32)
    square = -matmul(half_gen, half_gen)
    fourth = matmul(square, square)
    bound = 1.0001 * jnp.sqrt(jnp.max(jnp.sum(jnp.abs(fourth), axis=1)))
    factor = 2.0 / (2.0 + bound)
    rest = 1.0 - factor
    sum_ref[...] = factor * ((1.0 + rest) * eye - factor * square)
    power_ref[...] = rest * rest * eye - (2.0 * rest * factor) * square + factor * factor * fourth

    def going(state):
        step, left = state
        return jnp.logical_and(step < 24, left > SMALL)

    def body(state):
        step, left = state
        power = power_ref[...]
        sum_ref[...] += matmul(sum_ref[...], power)

        @pl.when(left * left > SMALL)
        def _():
            power_ref[...] = matmul(power, power)

        return step + 1, left * left

    def quick_going(state):
        return jnp.logical_and(bound < 16.0, going(state))

    def quick_body(state):
        step, left = state
        power = power_ref[...]
        both = by_parts(jnp.concatenate([sum_ref[...], power], axis=0), power)
        sum_ref[...] += both[:PAIR]
        power_ref[...] = both[PAIR:]
        return step + 1, left * left

    reach = bound / (2.0 + bound)
    state = lax.while_loop(quick_going, quick_body, (jnp.int32(0), reach * reach))
    lax.while_loop(going, body, state)
    result = 2.0 * matmul(eye + half_gen, sum_ref[...]) - eye
    share = PAIR // subs
    for i in range(subs):

        @pl.when(sub == i)
        def _():
            out_ref[...] = result[i * share : (i + 1) * share].astype(BF16)


def rotation_share(scale, me, packed):
    subs = packed.shape[0]
    return pl.pallas_call(
        functools.partial(rotation_kernel, scale, subs),
        out_shape=jax.ShapeDtypeStruct((PAIR // subs, PAIR), BF16),
        in_specs=[SMEM, VMEM],
        out_specs=VMEM,
        scratch_shapes=[pltpu.VMEM((PAIR, PAIR), F32), pltpu.VMEM((PAIR, PAIR), F32)],
        compiler_params=params(),
        name="rotation",
    )(me, packed)


def assemble(gathered_ref, me, slot):
    subs = PAIR // gathered_ref.shape[1]
    slots = gathered_ref.shape[0] // subs
    my_sub = me & (subs - 1)
    return jnp.concatenate(
        [gathered_ref[(i ^ my_sub) * slots + slot] for i in range(subs)], axis=0
    )


def rotate_kernel(first, earlier, place_ref, me_ref, gathered_ref, cols_ref, *refs):
    subs = PAIR // gathered_ref.shape[1]
    my_pair = me_ref[0] // subs
    image_refs, (out_ref, image_ref, diag_ref) = refs[: -3 - earlier], refs[-3:]
    for slot in range(gathered_ref.shape[0] // subs):
        p = my_pair ^ (first + slot)
        rotation = assemble(gathered_ref, me_ref[0], slot)
        places = [place_ref[2 * p + h] for h in (0, 1)]
        spot = pl.ds(pl.multiple_of(p * PAIR, PAIR), PAIR)
        cols = pair_columns(cols_ref, (), places)
        turned = jnp.dot(cols, rotation, preferred_element_type=F32).astype(BF16)
        out_ref[:, spot] = turned
        for k in range(3):
            image = pair_image(image_refs, k, places)
            moved = jnp.dot(image, rotation, preferred_element_type=F32).astype(BF16)
            image_ref[k, :, spot] = moved
            put_diag(diag_ref, k, 2 * p, turned, moved, True)


def rotate(place, me, gathered, cols, images, first, earlier):
    row_count, orb_count = cols.shape
    operands = [place, me, gathered, cols, *images]
    return pl.pallas_call(
        functools.partial(rotate_kernel, first, len(earlier)),
        out_shape=(
            jax.ShapeDtypeStruct((row_count, orb_count), BF16),
            jax.ShapeDtypeStruct((3, row_count, orb_count), BF16),
            jax.ShapeDtypeStruct((3, orb_count // HALF, HALF), F32),
        ),
        in_specs=[SMEM, SMEM] + [VMEM] * (2 + len(images) + len(earlier)),
        out_specs=(VMEM, VMEM, VMEM),
        cost_estimate=pl.CostEstimate(
            flops=8 * row_count * PAIR * PAIR * gathered.shape[0] * gathered.shape[1] // PAIR,
            bytes_accessed=8 * row_count * orb_count,
            transcendentals=0,
        ),
        input_output_aliases={len(operands) + i: i for i in range(len(earlier))},
        compiler_params=params(),
        name="rotate",
    )(*operands, *earlier)


def last_kernel(parts, place_ref, home_ref, me_ref, *refs):
    gathered_refs, (cols_ref, out_ref) = refs[:parts], refs[parts:]
    subs = PAIR // gathered_refs[0].shape[1]
    my_pair = me_ref[0] // subs
    done = 0
    for gathered_ref in gathered_refs:
        for slot in range(gathered_ref.shape[0] // subs):
            p = my_pair ^ done
            done += 1
            rotation = assemble(gathered_ref, me_ref[0], slot)
            places = [place_ref[2 * p + h] for h in (0, 1)]
            cols = pair_columns(cols_ref, (), places)
            turned = jnp.dot(cols, rotation, preferred_element_type=F32).astype(BF16)
            for h in (0, 1):
                home = pl.multiple_of(home_ref[2 * p + h] * HALF, HALF)
                out_ref[:, pl.ds(home, HALF)] = turned[:, h * HALF : (h + 1) * HALF]


def rotate_last(place, home, me, gathered, cols):
    row_count, orb_count = cols.shape
    rows = row_count // 2
    return pl.pallas_call(
        functools.partial(last_kernel, len(gathered)),
        out_shape=jax.ShapeDtypeStruct((row_count, orb_count), BF16),
        grid=(row_count // rows,),
        in_specs=[SMEM, SMEM, SMEM]
        + [pl.BlockSpec(part.shape, lambda r: (0, 0, 0)) for part in gathered]
        + [pl.BlockSpec((rows, orb_count), lambda r: (r, 0))],
        out_specs=pl.BlockSpec((rows, orb_count), lambda r: (r, 0)),
        compiler_params=params(),
        name="rotate_last",
    )(place, home, me, *gathered, cols)


def sum_beside(diag, makers):
    made = []
    hops = bits_of(lax.axis_size("orb"))
    for bit in range(hops):
        arrived = swap(diag, 1 << bit)
        for maker in makers.get(bit, ()):
            diag, arrived, product = lax.optimization_barrier((diag, arrived, maker(diag)))
            made.append(product)
        diag = diag + arrived
    return diag, made


def places_of(position, sub_bits, pair_bits):
    steps = [(bit, 1) for bit in range(1, sub_bits)] + [(sub_bits + 1, pair_bits - 1)]
    found = {}
    for low_bit, bits in steps:
        mine = (position >> low_bit) & ((1 << bits) - 1)
        found[low_bit] = [(mine ^ q).astype(jnp.uint32) for q in range(1 << bits)]
    return found


def pick(value, at):
    zero = jnp.uint32(0)
    start = (at,) + (zero,) * (value.ndim - 1)
    return lax.dynamic_slice(value, start, (1,) + value.shape[1:])[0]


def spread(value, places, low_bit, wire):
    ways = len(places)
    value = value.reshape((ways, -1) + value.shape[1:])
    pieces = [swap(pick(value, places[q]).astype(wire), q << low_bit) for q in range(1, ways)]
    own = pick(value, places[0])
    for piece in pieces:
        own = own + piece.astype(F32)
    return own


def reduce_pairs(keep, send, places, sub_bits):
    value = keep + swap(send, 1 << sub_bits).astype(F32)
    high = value.shape[0]
    for bit in range(1, sub_bits):
        rows = value.shape[1] // 2
        value = jnp.swapaxes(value.reshape(high, 2, rows, HALF), 0, 1)
        value = spread(value.reshape(2 * high, rows, HALF), places[bit], bit, F32)
    return spread(value, places[sub_bits + 1], sub_bits + 1, WIRE)[0]


def gather_bits(value, bits, low_bit):
    return jnp.concatenate(
        [value] + [swap(value, q << low_bit) for q in range(1, 1 << bits)], axis=0
    )


def gather_pairs(share, sub_bits, pair_bits):
    beside = 1 << sub_bits
    ways = 1 << (pair_bits - 1)
    away = {q: swap(share, q * 2 * beside) for q in range(ways - 1, 0, -1)}
    away[0] = share
    across = {q: swap(away[q], beside) for q in range(ways // 2)}
    across, away = lax.optimization_barrier((across, away))
    later = swap(jnp.concatenate([away[q] for q in range(ways // 2, ways)], axis=0), beside)
    near = jnp.concatenate([part[q] for q in range(ways // 2) for part in (away, across)], axis=0)
    for bit in range(sub_bits):
        near = gather_bits(near, 1, bit)
    later, near = lax.optimization_barrier((later, near))
    far = []
    for q in range(ways // 2, ways):
        far += [away[q], later[q - ways // 2 : q - ways // 2 + 1]]
    return near, jnp.concatenate(far, axis=0)


def per_device(orbitals, dipole_blocks, coupling_mask, matchings):
    row_count, orb_count = orbitals.shape
    count = lax.axis_size("orb")
    block_count = orb_count // HALF
    pair_count = orb_count // PAIR
    pair_bits = bits_of(pair_count)
    sub_bits = bits_of(count) - pair_bits
    basis_count = row_count * count
    block_rows = row_count // BLK
    last, first = edge_rows(orbitals)
    orbitals, matchings, last, first = lax.optimization_barrier(
        (orbitals, matchings, last, first)
    )
    position = lax.axis_index("orb").astype(jnp.int32)
    places = places_of(position, sub_bits, pair_bits)
    ident = jnp.arange(block_count, dtype=jnp.int32)
    held = [ident] + [matchings[r] for r in range(ROUNDS - 1)]
    spots = []
    for r in range(ROUNDS):
        found = jnp.where(matchings[r][:, None] == held[r][None, :], ident[None, :], 0)
        spots.append(jnp.sum(found, axis=1).astype(jnp.int32))
    forward = [(i, i + 1) for i in range(count - 1)]
    backward = [(i + 1, i) for i in range(count - 1)]
    orbitals, places, spots, me = lax.optimization_barrier(
        (orbitals, places, spots, position.reshape(1))
    )
    low = lax.ppermute(last, "orb", forward)
    high = lax.ppermute(first, "orb", backward)
    mask_full = jnp.stack(
        [coupling_mask[:, 0], jnp.ones((block_rows,), jnp.int32), coupling_mask[:, 1]], axis=1
    ).astype(BF16)
    blocks = jnp.transpose(
        dipole_blocks * mask_full[None, :, :, None, None], (1, 0, 3, 2, 4)
    ).reshape(block_rows, 3 * BLK, 3 * BLK)
    inner, diag = inner_images(blocks, orbitals)
    edge, diag = edge_images(blocks, orbitals, low, high, diag)

    cols, images = orbitals, (inner, edge)
    for round_index in range(ROUNDS):
        place = spots[round_index]
        splits = 4
        step = pair_count // splits

        def product(start, token):
            held_cols, _ = lax.optimization_barrier((cols, token))
            return pair_products(place, me, held_cols, images, start, step)

        made = [functools.partial(product, i * step) for i in range(splits)]
        makers = {0: made[:1], 1: made[1:3], 2: made[3:]}
        diag_sum, made = sum_beside(diag, makers)
        kept = [keep for keep, _ in made]
        came = [swap(send, 1) for _, send in made]
        keep, send = weigh(place, me, diag_sum, kept, came, sub_bits)
        own = reduce_pairs(keep, send, places, sub_bits)
        packed = own[None]
        for bit in range(sub_bits):
            packed = gather_bits(packed, 1, bit)
        share = rotation_share(0.01 / basis_count, me, packed)
        near, far = gather_pairs(share[None], sub_bits, pair_bits)
        if round_index + 1 < ROUNDS:
            earlier = rotate(place, me, near, cols, images, 0, ())
        for bit in range(sub_bits):
            far = gather_bits(far, 1, bit)
        if round_index + 1 < ROUNDS:
            half = pair_count // 2
            cols, moved, diag = rotate(place, me, far, cols, images, half, earlier)
            images = (moved,)
    return rotate_last(place, matchings[ROUNDS - 1], me, (near, far), cols)


def solution(mesh):
    in_specs = (
        P("orb", "groups"),
        P("groups", "orb", None, None, None),
        P("orb", "groups"),
        P("groups", None),
    )
    out_specs = P("orb", "groups")
    return jax.shard_map(
        per_device, mesh=mesh, in_specs=in_specs, out_specs=out_specs, check_vma=False
    )
```

```python
import functools

import jax
import jax.numpy as jnp
from jax import lax
from jax.experimental import pallas as pl
from jax.experimental.pallas import tpu as pltpu
from jax.sharding import PartitionSpec as P

HALF = 128
BLK = 128
ROUNDS = 2
PAIR = 2 * HALF
F32 = jnp.float32
BF16 = jnp.bfloat16
VMEM_LIMIT = 24 * 1024 * 1024
VMEM = pl.BlockSpec(memory_space=pltpu.VMEM)
SMEM = pl.BlockSpec(memory_space=pltpu.SMEM)
TILE = 512
SMALL = 1e-6
WIRE = BF16


def params(limit=VMEM_LIMIT):
    return pltpu.CompilerParams(vmem_limit_bytes=limit)


def bits_of(count):
    return count.bit_length() - 1


def bitrev(value, bits):
    return sum(((value >> j) & 1) << (bits - 1 - j) for j in range(bits))


def swap(block, distance):
    count = lax.axis_size("orb")
    return lax.ppermute(block, "orb", [(i, i ^ distance) for i in range(count)])


def put_diag(diag_ref, component, block, cols, image, first):
    total = jnp.sum(cols.astype(F32) * image.astype(F32), axis=0, keepdims=True)
    for half in range(total.shape[1] // HALF):
        spot = pl.ds(block + half, 1)
        piece = total[:, half * HALF : (half + 1) * HALF]
        if first:
            diag_ref[component, spot, :] = piece
        else:
            diag_ref[component, spot, :] += piece


def edge_rows_kernel(orbitals_ref, last_ref, first_ref, held_ref, sems):
    row_count = orbitals_ref.shape[0]
    spots = (orbitals_ref.at[row_count - BLK :], orbitals_ref.at[:BLK])
    loads = [pltpu.make_async_copy(spots[i], held_ref.at[i], sems.at[i]) for i in (0, 1)]
    stores = [
        pltpu.make_async_copy(held_ref.at[i], (last_ref, first_ref)[i], sems.at[2 + i])
        for i in (0, 1)
    ]
    for load in loads:
        load.start()
    for load, store in zip(loads, stores):
        load.wait()
        store.start()
    for store in stores:
        store.wait()


def edge_rows(orbitals):
    shape = jax.ShapeDtypeStruct((BLK, orbitals.shape[1]), BF16)
    hbm = pl.BlockSpec(memory_space=pltpu.HBM)
    return pl.pallas_call(
        edge_rows_kernel,
        out_shape=(shape, shape),
        in_specs=[hbm],
        out_specs=(hbm, hbm),
        scratch_shapes=[
            pltpu.VMEM((2, BLK, orbitals.shape[1]), BF16),
            pltpu.SemaphoreType.DMA((4,)),
        ],
        compiler_params=params(56 * 1024 * 1024),
        name="edge_rows",
    )(orbitals)


def inner_kernel(block_rows, blocks_ref, cols_ref, image_ref, diag_ref):
    for start in range(0, cols_ref.shape[1], TILE):
        tile = slice(start, start + TILE)
        for b in range(1, block_rows - 1):
            out = jnp.dot(
                blocks_ref[b],
                cols_ref[(b - 1) * BLK : (b + 2) * BLK, tile],
                preferred_element_type=F32,
            ).astype(BF16)
            own = cols_ref[b * BLK : (b + 1) * BLK, tile]
            for k in range(3):
                image = out[k * BLK : (k + 1) * BLK]
                image_ref[k, (b - 1) * BLK : b * BLK, tile] = image
                put_diag(diag_ref, k, start // HALF, own, image, b == 1)


def inner_images(blocks, orbitals):
    row_count, orb_count = orbitals.shape
    block_rows = row_count // BLK
    return pl.pallas_call(
        functools.partial(inner_kernel, block_rows),
        out_shape=(
            jax.ShapeDtypeStruct((3, row_count - 2 * BLK, orb_count), BF16),
            jax.ShapeDtypeStruct((3, orb_count // HALF, HALF), F32),
        ),
        in_specs=[VMEM, VMEM],
        out_specs=(VMEM, VMEM),
        compiler_params=params(),
        name="inner_images",
    )(blocks, orbitals)


def edge_kernel(block_rows, blocks_ref, cols_ref, low_ref, high_ref, start_ref, image_ref, diag_ref):
    diag_ref[...] = start_ref[...]
    for start in range(0, cols_ref.shape[1], TILE):
        tile = slice(start, start + TILE)
        for place, b in ((0, 0), (1, block_rows - 1)):
            if b == 0:
                window = jnp.concatenate([low_ref[:, tile], cols_ref[: 2 * BLK, tile]], axis=0)
            else:
                window = jnp.concatenate(
                    [cols_ref[(b - 1) * BLK :, tile], high_ref[:, tile]], axis=0
                )
            out = jnp.dot(blocks_ref[b], window, preferred_element_type=F32).astype(BF16)
            own = cols_ref[b * BLK : (b + 1) * BLK, tile]
            for k in range(3):
                image = out[k * BLK : (k + 1) * BLK]
                image_ref[k, place * BLK : (place + 1) * BLK, tile] = image
                put_diag(diag_ref, k, start // HALF, own, image, False)


def edge_images(blocks, orbitals, low, high, start):
    row_count, orb_count = orbitals.shape
    block_rows = row_count // BLK
    return pl.pallas_call(
        functools.partial(edge_kernel, block_rows),
        out_shape=(
            jax.ShapeDtypeStruct((3, 2 * BLK, orb_count), BF16),
            jax.ShapeDtypeStruct((3, orb_count // HALF, HALF), F32),
        ),
        in_specs=[VMEM] * 5,
        out_specs=(VMEM, VMEM),
        compiler_params=params(),
        name="edge_images",
    )(blocks, orbitals, low, high, start)


def lower_mask():
    rows = lax.broadcasted_iota(jnp.int32, (HALF, HALF), 0)
    cols = lax.broadcasted_iota(jnp.int32, (HALF, HALF), 1)
    return rows > cols


def pair_columns(ref, lead, places):
    return jnp.concatenate(
        [ref[lead + (slice(None), pl.ds(pl.multiple_of(at * HALF, HALF), HALF))] for at in places],
        axis=1,
    )


def pair_image(refs, component, places):
    pieces = [pair_columns(ref, (component,), places) for ref in refs]
    if len(pieces) == 1:
        return pieces[0]
    inner, edge = pieces
    return jnp.concatenate([edge[:BLK], inner, edge[BLK:]], axis=0)


def gram_kernel(first, place_ref, me_ref, cols_ref, *refs):
    image_refs, keep_ref, send_ref = refs[:-2], refs[-2], refs[-1]
    mine = (me_ref[0] & 1) == 0
    low = lower_mask()
    for i in range(keep_ref.shape[0]):
        places = [place_ref[2 * (first + i) + h] for h in (0, 1)]
        cols = pair_columns(cols_ref, (), places)
        images = jnp.concatenate([pair_image(image_refs, k, places) for k in range(3)], axis=1)
        mats = lax.dot_general(cols, images, (((0,), (0,)), ((), ())), preferred_element_type=F32)
        for k in range(3):
            mat = mats[:, k * PAIR : (k + 1) * PAIR]
            one, two = mat[:HALF, :HALF], mat[HALF:, HALF:]
            cross = mat[:HALF, HALF:] + mat[HALF:, :HALF].T
            within = jnp.where(low, one, two) + jnp.where(low, two, one).T
            keep_ref[i, k] = jnp.where(mine, cross, within)
            send_ref[i, k] = jnp.where(mine, within, cross)


def pair_products(place, me, cols, images, first, count):
    shape = jax.ShapeDtypeStruct((count, 3, HALF, HALF), F32)
    return pl.pallas_call(
        functools.partial(gram_kernel, first),
        out_shape=(shape, shape),
        in_specs=[SMEM, SMEM] + [VMEM] * (1 + len(images)),
        out_specs=(VMEM, VMEM),
        compiler_params=params(),
        name="pair_products",
    )(place, me, cols, *images)


def weight_kernel(sub_bits, stays, place_ref, me_ref, diag_ref, *refs):
    sums_refs, out_ref = refs[:-1], refs[-1]
    kept_refs, came_refs = sums_refs[: len(sums_refs) // 2], sums_refs[len(sums_refs) // 2 :]
    core = me_ref[0] & 1
    bit = (me_ref[0] >> sub_bits) & 1
    odd = bit if stays else 1 - bit
    rows = lax.broadcasted_iota(jnp.int32, (HALF, HALF), 0)
    cols = lax.broadcasted_iota(jnp.int32, (HALF, HALF), 1)
    low = jnp.where(rows > cols, 1, 0)
    col_first = jnp.maximum(low, 1 - core) > 0
    row_first = jnp.minimum(low, core) > 0
    step = kept_refs[0].shape[0]
    for j in range(out_ref.shape[0]):
        pair = 2 * j + odd
        i = 2 * j % step + odd
        kept_ref, came_ref = kept_refs[2 * j // step], came_refs[2 * j // step]
        halves = [
            [diag_ref[k, pl.ds(place_ref[2 * pair + h], 1), :] for k in range(3)] for h in (0, 1)
        ]
        first, second = [jnp.concatenate(half + half + half[:2], axis=0).T for half in halves]
        total = jnp.zeros((HALF, HALF), F32)
        for k in range(3):
            col = jnp.where(col_first, first[:, k : k + 1], second[:, k : k + 1])
            row = jnp.where(row_first, halves[0][k], halves[1][k])
            total += (kept_ref[i, k] + came_ref[i, k]) * (col - row)
        out_ref[j] = total.astype(out_ref.dtype)


def weigh(place, me, diag, kept, came, sub_bits, stays):
    high = sum(part.shape[0] for part in kept) // 2
    return pl.pallas_call(
        functools.partial(weight_kernel, sub_bits, stays),
        out_shape=jax.ShapeDtypeStruct((high, HALF, HALF), F32 if stays else BF16),
        in_specs=[SMEM, SMEM] + [VMEM] * (1 + 2 * len(kept)),
        out_specs=VMEM,
        compiler_params=params(),
        name="weigh",
    )(place, me, diag, *kept, *came)


def matmul(left, right):
    return jnp.dot(left, right, precision=lax.Precision.HIGHEST, preferred_element_type=F32)


def parts_of(value):
    high = value.astype(BF16)
    return high, (value - high.astype(F32)).astype(BF16)


def by_parts(left, right):
    left_high, left_low = parts_of(left)
    right_high, right_low = parts_of(right)
    rows = left.shape[0]
    both = jnp.dot(
        jnp.concatenate([left_high, left_low], axis=0), right_high, preferred_element_type=F32
    )
    return both[:rows] + (
        both[rows:] + jnp.dot(left_high, right_low, preferred_element_type=F32)
    )


def rotation_kernel(scale, subs, me_ref, packed_ref, out_ref, sum_ref, power_ref):
    sub = me_ref[0] & (subs - 1)
    pieces = [packed_ref[bitrev(i, bits_of(subs)) ^ sub] for i in range(subs)]
    packed = jnp.concatenate(pieces, axis=0) * scale
    cross, within = packed[:HALF], packed[HALF:]
    low = lower_mask()
    first = jnp.where(low, within, 0.0)
    second = jnp.where(low, 0.0, within)
    half_gen = jnp.concatenate(
        [
            jnp.concatenate([first - first.T, cross], axis=1),
            jnp.concatenate([-cross.T, second - second.T], axis=1),
        ],
        axis=0,
    )
    rows = lax.broadcasted_iota(jnp.int32, (PAIR, PAIR), 0)
    cols = lax.broadcasted_iota(jnp.int32, (PAIR, PAIR), 1)
    eye = jnp.where(rows == cols, 1.0, 0.0).astype(F32)
    square = -matmul(half_gen, half_gen)
    fourth = matmul(square, square)
    bound = 1.0001 * jnp.sqrt(jnp.max(jnp.sum(jnp.abs(fourth), axis=1)))
    factor = 2.0 / (2.0 + bound)
    rest = 1.0 - factor
    sum_ref[...] = factor * ((1.0 + rest) * eye - factor * square)
    power_ref[...] = rest * rest * eye - (2.0 * rest * factor) * square + factor * factor * fourth

    def going(state):
        step, left = state
        return jnp.logical_and(step < 24, left > SMALL)

    def body(state):
        step, left = state
        power = power_ref[...]
        sum_ref[...] += matmul(sum_ref[...], power)

        @pl.when(left * left > SMALL)
        def _():
            power_ref[...] = matmul(power, power)

        return step + 1, left * left

    def quick_going(state):
        return jnp.logical_and(bound < 16.0, going(state))

    def quick_body(state):
        step, left = state
        power = power_ref[...]
        both = by_parts(jnp.concatenate([sum_ref[...], power], axis=0), power)
        sum_ref[...] += both[:PAIR]
        power_ref[...] = both[PAIR:]
        return step + 1, left * left

    reach = bound / (2.0 + bound)
    state = lax.while_loop(quick_going, quick_body, (jnp.int32(0), reach * reach))
    lax.while_loop(going, body, state)
    result = 2.0 * matmul(eye + half_gen, sum_ref[...]) - eye
    share = PAIR // subs
    for i in range(subs):

        @pl.when(sub == i)
        def _():
            out_ref[...] = result[i * share : (i + 1) * share].astype(BF16)


def rotation_share(scale, me, packed):
    subs = packed.shape[0]
    return pl.pallas_call(
        functools.partial(rotation_kernel, scale, subs),
        out_shape=jax.ShapeDtypeStruct((PAIR // subs, PAIR), BF16),
        in_specs=[SMEM, VMEM],
        out_specs=VMEM,
        scratch_shapes=[pltpu.VMEM((PAIR, PAIR), F32), pltpu.VMEM((PAIR, PAIR), F32)],
        compiler_params=params(),
        name="rotation",
    )(me, packed)


def assemble(gathered_ref, me, slot):
    subs = PAIR // gathered_ref.shape[1]
    slots = gathered_ref.shape[0] // subs
    my_sub = me & (subs - 1)
    return jnp.concatenate(
        [gathered_ref[(i ^ my_sub) * slots + slot] for i in range(subs)], axis=0
    )


def rotate_kernel(first, earlier, place_ref, me_ref, gathered_ref, cols_ref, *refs):
    subs = PAIR // gathered_ref.shape[1]
    my_pair = me_ref[0] // subs
    image_refs, (out_ref, image_ref, diag_ref) = refs[: -3 - earlier], refs[-3:]
    for slot in range(gathered_ref.shape[0] // subs):
        p = my_pair ^ (first + slot)
        rotation = assemble(gathered_ref, me_ref[0], slot)
        places = [place_ref[2 * p + h] for h in (0, 1)]
        spot = pl.ds(pl.multiple_of(p * PAIR, PAIR), PAIR)
        cols = pair_columns(cols_ref, (), places)
        turned = jnp.dot(cols, rotation, preferred_element_type=F32).astype(BF16)
        out_ref[:, spot] = turned
        for k in range(3):
            image = pair_image(image_refs, k, places)
            moved = jnp.dot(image, rotation, preferred_element_type=F32).astype(BF16)
            image_ref[k, :, spot] = moved
            put_diag(diag_ref, k, 2 * p, turned, moved, True)


def rotate(place, me, gathered, cols, images, first, earlier):
    row_count, orb_count = cols.shape
    operands = [place, me, gathered, cols, *images]
    return pl.pallas_call(
        functools.partial(rotate_kernel, first, len(earlier)),
        out_shape=(
            jax.ShapeDtypeStruct((row_count, orb_count), BF16),
            jax.ShapeDtypeStruct((3, row_count, orb_count), BF16),
            jax.ShapeDtypeStruct((3, orb_count // HALF, HALF), F32),
        ),
        in_specs=[SMEM, SMEM] + [VMEM] * (2 + len(images) + len(earlier)),
        out_specs=(VMEM, VMEM, VMEM),
        cost_estimate=pl.CostEstimate(
            flops=8 * row_count * PAIR * PAIR * gathered.shape[0] * gathered.shape[1] // PAIR,
            bytes_accessed=8 * row_count * orb_count,
            transcendentals=0,
        ),
        input_output_aliases={len(operands) + i: i for i in range(len(earlier))},
        compiler_params=params(),
        name="rotate",
    )(*operands, *earlier)


def last_kernel(parts, place_ref, home_ref, me_ref, *refs):
    gathered_refs, (cols_ref, out_ref) = refs[:parts], refs[parts:]
    subs = PAIR // gathered_refs[0].shape[1]
    my_pair = me_ref[0] // subs
    done = 0
    for gathered_ref in gathered_refs:
        for slot in range(gathered_ref.shape[0] // subs):
            p = my_pair ^ done
            done += 1
            rotation = assemble(gathered_ref, me_ref[0], slot)
            places = [place_ref[2 * p + h] for h in (0, 1)]
            cols = pair_columns(cols_ref, (), places)
            turned = jnp.dot(cols, rotation, preferred_element_type=F32).astype(BF16)
            for h in (0, 1):
                home = pl.multiple_of(home_ref[2 * p + h] * HALF, HALF)
                out_ref[:, pl.ds(home, HALF)] = turned[:, h * HALF : (h + 1) * HALF]


def rotate_last(place, home, me, gathered, cols):
    row_count, orb_count = cols.shape
    rows = row_count // 2
    return pl.pallas_call(
        functools.partial(last_kernel, len(gathered)),
        out_shape=jax.ShapeDtypeStruct((row_count, orb_count), BF16),
        grid=(row_count // rows,),
        in_specs=[SMEM, SMEM, SMEM]
        + [pl.BlockSpec(part.shape, lambda r: (0, 0, 0)) for part in gathered]
        + [pl.BlockSpec((rows, orb_count), lambda r: (r, 0))],
        out_specs=pl.BlockSpec((rows, orb_count), lambda r: (r, 0)),
        compiler_params=params(),
        name="rotate_last",
    )(place, home, me, *gathered, cols)


def sum_beside(diag, makers):
    made = []
    hops = bits_of(lax.axis_size("orb"))
    for bit in range(hops):
        arrived = swap(diag, 1 << bit)
        products, token = [], diag
        for maker in makers.get(bit, ()):
            products.append(maker(token))
            token = products[-1][0]
        diag, arrived, products = lax.optimization_barrier((diag, arrived, products))
        made += products
        diag = diag + arrived
    return diag, made


def places_of(position, sub_bits, pair_bits):
    steps = [(bit, 1) for bit in range(1, sub_bits)] + [(sub_bits + 1, pair_bits - 1)]
    found = {}
    for low_bit, bits in steps:
        mine = (position >> low_bit) & ((1 << bits) - 1)
        found[low_bit] = [(mine ^ q).astype(jnp.uint32) for q in range(1 << bits)]
    return found


def pick(value, at):
    zero = jnp.uint32(0)
    start = (at,) + (zero,) * (value.ndim - 1)
    return lax.dynamic_slice(value, start, (1,) + value.shape[1:])[0]


def spread(value, places, low_bit, wire):
    ways = len(places)
    value = value.reshape((ways, -1) + value.shape[1:])
    pieces = [swap(pick(value, places[q]).astype(wire), q << low_bit) for q in range(1, ways)]
    own = pick(value, places[0])
    for piece in pieces:
        own = own + piece.astype(F32)
    return own


def reduce_pairs(value, places, sub_bits):
    high = value.shape[0]
    for bit in range(1, sub_bits):
        rows = value.shape[1] // 2
        value = jnp.swapaxes(value.reshape(high, 2, rows, HALF), 0, 1)
        value = spread(value.reshape(2 * high, rows, HALF), places[bit], bit, F32)
    return spread(value, places[sub_bits + 1], sub_bits + 1, WIRE)[0]


def gather_bits(value, bits, low_bit):
    return jnp.concatenate(
        [value] + [swap(value, q << low_bit) for q in range(1, 1 << bits)], axis=0
    )


def gather_pairs(share, sub_bits, pair_bits):
    beside = 1 << sub_bits
    ways = 1 << (pair_bits - 1)
    away = {q: swap(share, q * 2 * beside) for q in range(ways - 1, 0, -1)}
    away[0] = share
    across = {q: swap(away[q], beside) for q in range(ways // 2)}
    across, away = lax.optimization_barrier((across, away))
    later = swap(jnp.concatenate([away[q] for q in range(ways // 2, ways)], axis=0), beside)
    near = jnp.concatenate([part[q] for q in range(ways // 2) for part in (away, across)], axis=0)
    for bit in range(sub_bits):
        near = gather_bits(near, 1, bit)
    later, near = lax.optimization_barrier((later, near))
    far = []
    for q in range(ways // 2, ways):
        far += [away[q], later[q - ways // 2 : q - ways // 2 + 1]]
    return near, jnp.concatenate(far, axis=0)


def per_device(orbitals, dipole_blocks, coupling_mask, matchings):
    row_count, orb_count = orbitals.shape
    count = lax.axis_size("orb")
    block_count = orb_count // HALF
    pair_count = orb_count // PAIR
    pair_bits = bits_of(pair_count)
    sub_bits = bits_of(count) - pair_bits
    basis_count = row_count * count
    block_rows = row_count // BLK
    last, first = edge_rows(orbitals)
    orbitals, matchings, last, first = lax.optimization_barrier(
        (orbitals, matchings, last, first)
    )
    position = lax.axis_index("orb").astype(jnp.int32)
    places = places_of(position, sub_bits, pair_bits)
    ident = jnp.arange(block_count, dtype=jnp.int32)
    held = [ident] + [matchings[r] for r in range(ROUNDS - 1)]
    spots = []
    for r in range(ROUNDS):
        found = jnp.where(matchings[r][:, None] == held[r][None, :], ident[None, :], 0)
        spots.append(jnp.sum(found, axis=1).astype(jnp.int32))
    forward = [(i, i + 1) for i in range(count - 1)]
    backward = [(i + 1, i) for i in range(count - 1)]
    orbitals, places, spots, me = lax.optimization_barrier(
        (orbitals, places, spots, position.reshape(1))
    )
    low = lax.ppermute(last, "orb", forward)
    high = lax.ppermute(first, "orb", backward)
    mask_full = jnp.stack(
        [coupling_mask[:, 0], jnp.ones((block_rows,), jnp.int32), coupling_mask[:, 1]], axis=1
    ).astype(BF16)
    blocks = jnp.transpose(
        dipole_blocks * mask_full[None, :, :, None, None], (1, 0, 3, 2, 4)
    ).reshape(block_rows, 3 * BLK, 3 * BLK)
    inner, diag = inner_images(blocks, orbitals)
    edge, diag = edge_images(blocks, orbitals, low, high, diag)

    cols, images = orbitals, (inner, edge)
    for round_index in range(ROUNDS):
        place = spots[round_index]
        splits = 4
        step = pair_count // splits

        def product(start, token):
            held_cols, _ = lax.optimization_barrier((cols, token))
            return pair_products(place, me, held_cols, images, start, step)

        made = [functools.partial(product, i * step) for i in range(splits)]
        makers = {0: made[:1], 1: made[1:3], 2: made[3:]}
        diag_sum, made = sum_beside(diag, makers)
        kept = [keep for keep, _ in made]
        came = [swap(send, 1) for _, send in made]
        send = weigh(place, me, diag_sum, kept, came, sub_bits, False)
        across = swap(send, 1 << sub_bits)
        keep = weigh(place, me, diag_sum, kept, came, sub_bits, True)
        across, keep = lax.optimization_barrier((across, keep))
        own = reduce_pairs(keep + across.astype(F32), places, sub_bits)
        packed = own[None]
        for bit in range(sub_bits):
            packed = gather_bits(packed, 1, bit)
        share = rotation_share(0.01 / basis_count, me, packed)
        near, far = gather_pairs(share[None], sub_bits, pair_bits)
        if round_index + 1 < ROUNDS:
            earlier = rotate(place, me, near, cols, images, 0, ())
        for bit in range(sub_bits):
            far = gather_bits(far, 1, bit)
        if round_index + 1 < ROUNDS:
            half = pair_count // 2
            cols, moved, diag = rotate(place, me, far, cols, images, half, earlier)
            images = (moved,)
    return rotate_last(place, matchings[ROUNDS - 1], me, (near, far), cols)


def solution(mesh):
    in_specs = (
        P("orb", "groups"),
        P("groups", "orb", None, None, None),
        P("orb", "groups"),
        P("groups", None),
    )
    out_specs = P("orb", "groups")
    return jax.shard_map(
        per_device, mesh=mesh, in_specs=in_specs, out_specs=out_specs, check_vma=False
    )
```

```python
import functools

import jax
import jax.numpy as jnp
from jax import lax
from jax.experimental import pallas as pl
from jax.experimental.pallas import tpu as pltpu
from jax.sharding import PartitionSpec as P

HALF = 128
BLK = 128
ROUNDS = 2
PAIR = 2 * HALF
F32 = jnp.float32
BF16 = jnp.bfloat16
VMEM_LIMIT = 24 * 1024 * 1024
VMEM = pl.BlockSpec(memory_space=pltpu.VMEM)
SMEM = pl.BlockSpec(memory_space=pltpu.SMEM)
TILE = 512
SMALL = 1e-6
WIRE = BF16


def params(limit=VMEM_LIMIT):
    return pltpu.CompilerParams(vmem_limit_bytes=limit)


def bits_of(count):
    return count.bit_length() - 1


def bitrev(value, bits):
    return sum(((value >> j) & 1) << (bits - 1 - j) for j in range(bits))


def swap(block, distance):
    count = lax.axis_size("orb")
    return lax.ppermute(block, "orb", [(i, i ^ distance) for i in range(count)])


def put_diag(diag_ref, component, block, cols, image, first):
    total = jnp.sum(cols.astype(F32) * image.astype(F32), axis=0, keepdims=True)
    for half in range(total.shape[1] // HALF):
        spot = pl.ds(block + half, 1)
        piece = total[:, half * HALF : (half + 1) * HALF]
        if first:
            diag_ref[component, spot, :] = piece
        else:
            diag_ref[component, spot, :] += piece


def edge_rows_kernel(me_ref, orbitals_ref, chip_ref, next_ref, held_ref, sems):
    span = orbitals_ref.shape[0] - BLK
    even = 1 - (me_ref[0] & 1)
    starts = (even * span, (1 - even) * span)
    loads = [
        pltpu.make_async_copy(
            orbitals_ref.at[pl.ds(pl.multiple_of(starts[i], BLK), BLK)], held_ref.at[i], sems.at[i]
        )
        for i in (0, 1)
    ]
    stores = [
        pltpu.make_async_copy(held_ref.at[i], (chip_ref, next_ref)[i], sems.at[2 + i])
        for i in (0, 1)
    ]
    for load in loads:
        load.start()
    for load, store in zip(loads, stores):
        load.wait()
        store.start()
    for store in stores:
        store.wait()


def edge_rows(me, orbitals):
    shape = jax.ShapeDtypeStruct((BLK, orbitals.shape[1]), BF16)
    hbm = pl.BlockSpec(memory_space=pltpu.HBM)
    return pl.pallas_call(
        edge_rows_kernel,
        out_shape=(shape, shape),
        in_specs=[SMEM, hbm],
        out_specs=(hbm, hbm),
        scratch_shapes=[
            pltpu.VMEM((2, BLK, orbitals.shape[1]), BF16),
            pltpu.SemaphoreType.DMA((4,)),
        ],
        compiler_params=params(56 * 1024 * 1024),
        name="edge_rows",
    )(me, orbitals)


def put_images(blocks_ref, cols_ref, window, b, tile, image_ref, diag_ref, first):
    out = jnp.dot(blocks_ref[b], window, preferred_element_type=F32).astype(BF16)
    own = cols_ref[b * BLK : (b + 1) * BLK, tile]
    for k in range(3):
        image = out[k * BLK : (k + 1) * BLK]
        image_ref[k, b * BLK : (b + 1) * BLK, tile] = image
        put_diag(diag_ref, k, tile.start // HALF, own, image, first)


def inner_kernel(block_rows, blocks_ref, cols_ref, image_ref, diag_ref):
    for start in range(0, cols_ref.shape[1], TILE):
        tile = slice(start, start + TILE)
        for b in range(1, block_rows - 1):
            window = cols_ref[(b - 1) * BLK : (b + 2) * BLK, tile]
            put_images(blocks_ref, cols_ref, window, b, tile, image_ref, diag_ref, b == 1)


def image_shapes(orbitals):
    row_count, orb_count = orbitals.shape
    return (
        jax.ShapeDtypeStruct((3, row_count, orb_count), BF16),
        jax.ShapeDtypeStruct((3, orb_count // HALF, HALF), F32),
    )


def inner_images(blocks, orbitals):
    return pl.pallas_call(
        functools.partial(inner_kernel, orbitals.shape[0] // BLK),
        out_shape=image_shapes(orbitals),
        in_specs=[VMEM, VMEM],
        out_specs=(VMEM, VMEM),
        compiler_params=params(),
        name="inner_images",
    )(blocks, orbitals)


def edge_kernel(
    block_rows, on_chip, me_ref, blocks_ref, cols_ref, came_ref, *refs
):
    old_diag_ref, image_ref, diag_ref = refs[1:]
    even = (me_ref[0] & 1) == 0
    last = even if on_chip else jnp.logical_not(even)
    diag_ref[...] = old_diag_ref[...]

    def put(b):
        for start in range(0, cols_ref.shape[1], TILE):
            tile = slice(start, start + TILE)
            if b == 0:
                pieces = [came_ref[:, tile], cols_ref[: 2 * BLK, tile]]
            else:
                pieces = [cols_ref[(b - 1) * BLK :, tile], came_ref[:, tile]]
            window = jnp.concatenate(pieces, axis=0)
            put_images(blocks_ref, cols_ref, window, b, tile, image_ref, diag_ref, False)

    @pl.when(last)
    def _():
        put(block_rows - 1)

    @pl.when(jnp.logical_not(last))
    def _():
        put(0)


def edge_images(me, blocks, orbitals, came, images, diag, on_chip):
    return pl.pallas_call(
        functools.partial(edge_kernel, orbitals.shape[0] // BLK, on_chip),
        out_shape=image_shapes(orbitals),
        in_specs=[SMEM] + [VMEM] * 5,
        out_specs=(VMEM, VMEM),
        input_output_aliases={4: 0, 5: 1},
        compiler_params=params(),
        name="edge_images",
    )(me, blocks, orbitals, came, images, diag)


def lower_mask():
    rows = lax.broadcasted_iota(jnp.int32, (HALF, HALF), 0)
    cols = lax.broadcasted_iota(jnp.int32, (HALF, HALF), 1)
    return rows > cols


def pair_columns(ref, lead, places):
    return jnp.concatenate(
        [ref[lead + (slice(None), pl.ds(pl.multiple_of(at * HALF, HALF), HALF))] for at in places],
        axis=1,
    )


def gram_kernel(first, place_ref, me_ref, cols_ref, image_ref, keep_ref, send_ref):
    mine = (me_ref[0] & 1) == 0
    low = lower_mask()
    for i in range(keep_ref.shape[0]):
        places = [place_ref[2 * (first + i) + h] for h in (0, 1)]
        cols = pair_columns(cols_ref, (), places)
        images = jnp.concatenate([pair_columns(image_ref, (k,), places) for k in range(3)], axis=1)
        mats = lax.dot_general(cols, images, (((0,), (0,)), ((), ())), preferred_element_type=F32)
        for k in range(3):
            mat = mats[:, k * PAIR : (k + 1) * PAIR]
            one, two = mat[:HALF, :HALF], mat[HALF:, HALF:]
            cross = mat[:HALF, HALF:] + mat[HALF:, :HALF].T
            within = jnp.where(low, one, two) + jnp.where(low, two, one).T
            keep_ref[i, k] = jnp.where(mine, cross, within)
            send_ref[i, k] = jnp.where(mine, within, cross)


def pair_products(place, me, cols, images, first, count):
    shape = jax.ShapeDtypeStruct((count, 3, HALF, HALF), F32)
    return pl.pallas_call(
        functools.partial(gram_kernel, first),
        out_shape=(shape, shape),
        in_specs=[SMEM, SMEM, VMEM, VMEM],
        out_specs=(VMEM, VMEM),
        compiler_params=params(),
        name="pair_products",
    )(place, me, cols, images)


def weight_kernel(sub_bits, stays, place_ref, me_ref, diag_ref, *refs):
    sums_refs, out_ref = refs[:-1], refs[-1]
    kept_refs, came_refs = sums_refs[: len(sums_refs) // 2], sums_refs[len(sums_refs) // 2 :]
    core = me_ref[0] & 1
    bit = (me_ref[0] >> sub_bits) & 1
    odd = bit if stays else 1 - bit
    rows = lax.broadcasted_iota(jnp.int32, (HALF, HALF), 0)
    cols = lax.broadcasted_iota(jnp.int32, (HALF, HALF), 1)
    low = jnp.where(rows > cols, 1, 0)
    col_first = jnp.maximum(low, 1 - core) > 0
    row_first = jnp.minimum(low, core) > 0
    step = kept_refs[0].shape[0]
    for j in range(out_ref.shape[0]):
        pair = 2 * j + odd
        i = 2 * j % step + odd
        kept_ref, came_ref = kept_refs[2 * j // step], came_refs[2 * j // step]
        halves = [
            [diag_ref[k, pl.ds(place_ref[2 * pair + h], 1), :] for k in range(3)] for h in (0, 1)
        ]
        first, second = [jnp.concatenate(half + half + half[:2], axis=0).T for half in halves]
        total = jnp.zeros((HALF, HALF), F32)
        for k in range(3):
            col = jnp.where(col_first, first[:, k : k + 1], second[:, k : k + 1])
            row = jnp.where(row_first, halves[0][k], halves[1][k])
            total += (kept_ref[i, k] + came_ref[i, k]) * (col - row)
        out_ref[j] = total.astype(out_ref.dtype)


def weigh(place, me, diag, kept, came, sub_bits, stays):
    high = sum(part.shape[0] for part in kept) // 2
    return pl.pallas_call(
        functools.partial(weight_kernel, sub_bits, stays),
        out_shape=jax.ShapeDtypeStruct((high, HALF, HALF), F32 if stays else BF16),
        in_specs=[SMEM, SMEM] + [VMEM] * (1 + 2 * len(kept)),
        out_specs=VMEM,
        compiler_params=params(),
        name="weigh",
    )(place, me, diag, *kept, *came)


def matmul(left, right):
    return jnp.dot(left, right, precision=lax.Precision.HIGHEST, preferred_element_type=F32)


def parts_of(value):
    high = value.astype(BF16)
    return high, (value - high.astype(F32)).astype(BF16)


def by_parts(left, right):
    left_high, left_low = parts_of(left)
    right_high, right_low = parts_of(right)
    rows = left.shape[0]
    both = jnp.dot(
        jnp.concatenate([left_high, left_low], axis=0), right_high, preferred_element_type=F32
    )
    return both[:rows] + (
        both[rows:] + jnp.dot(left_high, right_low, preferred_element_type=F32)
    )


def rotation_kernel(scale, subs, me_ref, packed_ref, out_ref, sum_ref, power_ref):
    sub = me_ref[0] & (subs - 1)
    pieces = [packed_ref[bitrev(i, bits_of(subs)) ^ sub] for i in range(subs)]
    packed = jnp.concatenate(pieces, axis=0) * scale
    cross, within = packed[:HALF], packed[HALF:]
    low = lower_mask()
    first = jnp.where(low, within, 0.0)
    second = jnp.where(low, 0.0, within)
    half_gen = jnp.concatenate(
        [
            jnp.concatenate([first - first.T, cross], axis=1),
            jnp.concatenate([-cross.T, second - second.T], axis=1),
        ],
        axis=0,
    )
    rows = lax.broadcasted_iota(jnp.int32, (PAIR, PAIR), 0)
    cols = lax.broadcasted_iota(jnp.int32, (PAIR, PAIR), 1)
    eye = jnp.where(rows == cols, 1.0, 0.0).astype(F32)
    square = -matmul(half_gen, half_gen)
    fourth = matmul(square, square)
    bound = 1.0001 * jnp.sqrt(jnp.max(jnp.sum(jnp.abs(fourth), axis=1)))
    factor = 2.0 / (2.0 + bound)
    rest = 1.0 - factor
    sum_ref[...] = factor * ((1.0 + rest) * eye - factor * square)
    power_ref[...] = rest * rest * eye - (2.0 * rest * factor) * square + factor * factor * fourth

    def going(state):
        step, left = state
        return jnp.logical_and(step < 24, left > SMALL)

    def body(state):
        step, left = state
        power = power_ref[...]
        sum_ref[...] += matmul(sum_ref[...], power)

        @pl.when(left * left > SMALL)
        def _():
            power_ref[...] = matmul(power, power)

        return step + 1, left * left

    def quick_going(state):
        return jnp.logical_and(bound < 16.0, going(state))

    def quick_body(state):
        step, left = state
        power = power_ref[...]
        both = by_parts(jnp.concatenate([sum_ref[...], power], axis=0), power)
        sum_ref[...] += both[:PAIR]
        power_ref[...] = both[PAIR:]
        return step + 1, left * left

    reach = bound / (2.0 + bound)
    state = lax.while_loop(quick_going, quick_body, (jnp.int32(0), reach * reach))
    lax.while_loop(going, body, state)
    result = 2.0 * matmul(eye + half_gen, sum_ref[...]) - eye
    share = PAIR // subs
    for i in range(subs):

        @pl.when(sub == i)
        def _():
            out_ref[...] = result[i * share : (i + 1) * share].astype(BF16)


def rotation_share(scale, me, packed):
    subs = packed.shape[0]
    return pl.pallas_call(
        functools.partial(rotation_kernel, scale, subs),
        out_shape=jax.ShapeDtypeStruct((PAIR // subs, PAIR), BF16),
        in_specs=[SMEM, VMEM],
        out_specs=VMEM,
        scratch_shapes=[pltpu.VMEM((PAIR, PAIR), F32), pltpu.VMEM((PAIR, PAIR), F32)],
        compiler_params=params(),
        name="rotation",
    )(me, packed)


def assemble(gathered_ref, me, slot):
    subs = PAIR // gathered_ref.shape[1]
    slots = gathered_ref.shape[0] // subs
    my_sub = me & (subs - 1)
    return jnp.concatenate(
        [gathered_ref[(i ^ my_sub) * slots + slot] for i in range(subs)], axis=0
    )


def rotate_kernel(first, place_ref, me_ref, gathered_ref, cols_ref, old_ref, *refs):
    subs = PAIR // gathered_ref.shape[1]
    my_pair = me_ref[0] // subs
    out_ref, image_ref, diag_ref = refs[-3:]
    for slot in range(gathered_ref.shape[0] // subs):
        p = my_pair ^ (first + slot)
        rotation = assemble(gathered_ref, me_ref[0], slot)
        places = [place_ref[2 * p + h] for h in (0, 1)]
        spot = pl.ds(pl.multiple_of(p * PAIR, PAIR), PAIR)
        cols = pair_columns(cols_ref, (), places)
        turned = jnp.dot(cols, rotation, preferred_element_type=F32).astype(BF16)
        out_ref[:, spot] = turned
        for k in range(3):
            image = pair_columns(old_ref, (k,), places)
            moved = jnp.dot(image, rotation, preferred_element_type=F32).astype(BF16)
            image_ref[k, :, spot] = moved
            put_diag(diag_ref, k, 2 * p, turned, moved, True)


def rotate(place, me, gathered, cols, images, first, earlier):
    row_count, orb_count = cols.shape
    operands = [place, me, gathered, cols, images]
    return pl.pallas_call(
        functools.partial(rotate_kernel, first),
        out_shape=(
            jax.ShapeDtypeStruct((row_count, orb_count), BF16),
            jax.ShapeDtypeStruct((3, row_count, orb_count), BF16),
            jax.ShapeDtypeStruct((3, orb_count // HALF, HALF), F32),
        ),
        in_specs=[SMEM, SMEM] + [VMEM] * (3 + len(earlier)),
        out_specs=(VMEM, VMEM, VMEM),
        cost_estimate=pl.CostEstimate(
            flops=8 * row_count * PAIR * PAIR * gathered.shape[0] * gathered.shape[1] // PAIR,
            bytes_accessed=8 * row_count * orb_count,
            transcendentals=0,
        ),
        input_output_aliases={len(operands) + i: i for i in range(len(earlier))},
        compiler_params=params(),
        name="rotate",
    )(*operands, *earlier)


def turn_kernel(place_ref, me_ref, gathered_ref, cols_ref, out_ref):
    subs = PAIR // gathered_ref.shape[1]
    for slot in range(gathered_ref.shape[0] // subs):
        p = (me_ref[0] // subs) ^ slot
        rotation = assemble(gathered_ref, me_ref[0], slot)
        cols = pair_columns(cols_ref, (), [place_ref[2 * p + h] for h in (0, 1)])
        turned = jnp.dot(cols, rotation, preferred_element_type=F32).astype(BF16)
        out_ref[:, slot * PAIR : (slot + 1) * PAIR] = turned


def turn_near(place, me, gathered, cols):
    row_count = cols.shape[0]
    subs = PAIR // gathered.shape[1]
    slots = gathered.shape[0] // subs
    return pl.pallas_call(
        turn_kernel,
        out_shape=jax.ShapeDtypeStruct((row_count, slots * PAIR), BF16),
        in_specs=[SMEM, SMEM, VMEM, VMEM],
        out_specs=VMEM,
        compiler_params=params(),
        name="turn_near",
    )(place, me, gathered, cols)


def last_kernel(
    place_ref, home_ref, me_ref, turned_ref, gathered_ref, cols_ref, out_ref, held_ref, sems
):
    subs = PAIR // gathered_ref.shape[1]
    near = turned_ref.shape[1] // PAIR
    copies = []
    for slot in range(near + gathered_ref.shape[0] // subs):
        p = (me_ref[0] // subs) ^ slot
        if slot < near:
            source_ref, start = turned_ref, slot * PAIR
        else:
            source_ref, start = held_ref, (slot - near) * PAIR
            rotation = assemble(gathered_ref, me_ref[0], slot - near)
            cols = pair_columns(cols_ref, (), [place_ref[2 * p + h] for h in (0, 1)])
            turned = jnp.dot(cols, rotation, preferred_element_type=F32).astype(BF16)
            held_ref[:, start : start + PAIR] = turned
        for h in (0, 1):
            home = pl.multiple_of(home_ref[2 * p + h] * HALF, HALF)
            copies.append(
                pltpu.make_async_copy(
                    source_ref.at[:, pl.ds(start + h * HALF, HALF)],
                    out_ref.at[:, pl.ds(home, HALF)],
                    sems.at[2 * slot + h],
                )
            )
            copies[-1].start()
    for copy in copies:
        copy.wait()


def rotate_last(place, home, me, turned, gathered, cols):
    row_count, orb_count = cols.shape
    return pl.pallas_call(
        last_kernel,
        out_shape=jax.ShapeDtypeStruct((row_count, orb_count), BF16),
        in_specs=[SMEM, SMEM, SMEM, VMEM, VMEM, VMEM],
        out_specs=pl.BlockSpec(memory_space=pltpu.HBM),
        scratch_shapes=[
            pltpu.VMEM((row_count, orb_count - turned.shape[1]), BF16),
            pltpu.SemaphoreType.DMA((orb_count // HALF,)),
        ],
        compiler_params=params(),
        name="rotate_last",
    )(place, home, me, turned, gathered, cols)


def sum_beside(diag, makers):
    made = []
    hops = bits_of(lax.axis_size("orb"))
    for bit in range(hops):
        arrived = swap(diag, 1 << bit)
        products, token = [], diag
        for maker in makers.get(bit, ()):
            products.append(maker(token))
            token = products[-1][0]
        diag, arrived, products = lax.optimization_barrier((diag, arrived, products))
        made += products
        diag = diag + arrived
    return diag, made


def places_of(position, sub_bits, pair_bits):
    steps = [(bit, 1) for bit in range(1, sub_bits)] + [(sub_bits + 1, pair_bits - 1)]
    found = {}
    for low_bit, bits in steps:
        mine = (position >> low_bit) & ((1 << bits) - 1)
        found[low_bit] = [(mine ^ q).astype(jnp.uint32) for q in range(1 << bits)]
    return found


def pick(value, at):
    zero = jnp.uint32(0)
    start = (at,) + (zero,) * (value.ndim - 1)
    return lax.dynamic_slice(value, start, (1,) + value.shape[1:])[0]


def spread(value, places, low_bit, wire):
    ways = len(places)
    value = value.reshape((ways, -1) + value.shape[1:])
    pieces = [
        swap(pick(value, places[q]).astype(wire), q << low_bit) for q in range(ways - 1, 0, -1)
    ]
    own = pick(value, places[0])
    for piece in pieces:
        own = own + piece.astype(F32)
    return own


def reduce_pairs(value, places, sub_bits):
    high = value.shape[0]
    for bit in range(1, sub_bits):
        rows = value.shape[1] // 2
        value = jnp.swapaxes(value.reshape(high, 2, rows, HALF), 0, 1)
        value = spread(value.reshape(2 * high, rows, HALF), places[bit], bit, F32)
    return spread(value, places[sub_bits + 1], sub_bits + 1, WIRE)[0]


def gather_bits(value, bits, low_bit):
    return jnp.concatenate(
        [value] + [swap(value, q << low_bit) for q in range(1, 1 << bits)], axis=0
    )


def gather_pairs(share, sub_bits, pair_bits):
    beside = 1 << sub_bits
    ways = 1 << (pair_bits - 1)
    away = {q: swap(share, q * 2 * beside) for q in range(ways - 1, 0, -1)}
    away[0] = share
    across = {q: swap(away[q], beside) for q in range(ways // 2)}
    across, away = lax.optimization_barrier((across, away))
    later = swap(jnp.concatenate([away[q] for q in range(ways // 2, ways)], axis=0), beside)
    near = jnp.concatenate([part[q] for q in range(ways // 2) for part in (away, across)], axis=0)
    for bit in range(sub_bits):
        near = gather_bits(near, 1, bit)
    later, near = lax.optimization_barrier((later, near))
    far = []
    for q in range(ways // 2, ways):
        far += [away[q], later[q - ways // 2 : q - ways // 2 + 1]]
    return near, jnp.concatenate(far, axis=0)


def per_device(orbitals, dipole_blocks, coupling_mask, matchings):
    row_count, orb_count = orbitals.shape
    count = lax.axis_size("orb")
    block_count = orb_count // HALF
    pair_count = orb_count // PAIR
    pair_bits = bits_of(pair_count)
    sub_bits = bits_of(count) - pair_bits
    basis_count = row_count * count
    block_rows = row_count // BLK
    position = lax.axis_index("orb").astype(jnp.int32)
    for_chip, for_next = edge_rows(position.reshape(1), orbitals)
    from_chip = swap(for_chip, 1)
    joints = [(i, i + 1) for i in range(1, count - 1, 2)]
    from_next = lax.ppermute(for_next, "orb", joints + [(j, i) for i, j in joints])
    orbitals, matchings, for_next = lax.optimization_barrier((orbitals, matchings, for_next))
    places = places_of(position, sub_bits, pair_bits)
    ident = jnp.arange(block_count, dtype=jnp.int32)
    held = [ident] + [matchings[r] for r in range(ROUNDS - 1)]
    spots = []
    for r in range(ROUNDS):
        found = jnp.where(matchings[r][:, None] == held[r][None, :], ident[None, :], 0)
        spots.append(jnp.sum(found, axis=1).astype(jnp.int32))
    orbitals, places, spots, me = lax.optimization_barrier(
        (orbitals, places, spots, position.reshape(1))
    )

    mask_full = jnp.stack(
        [coupling_mask[:, 0], jnp.ones((block_rows,), jnp.int32), coupling_mask[:, 1]], axis=1
    ).astype(BF16)
    blocks = jnp.transpose(
        dipole_blocks * mask_full[None, :, :, None, None], (1, 0, 3, 2, 4)
    ).reshape(block_rows, 3 * BLK, 3 * BLK)
    images, diag = inner_images(blocks, orbitals)
    images, diag = edge_images(me, blocks, orbitals, from_chip, images, diag, True)
    from_next, images, diag = lax.optimization_barrier((from_next, images, diag))
    images, diag = edge_images(me, blocks, orbitals, from_next, images, diag, False)
    cols = orbitals
    for round_index in range(ROUNDS):
        place = spots[round_index]
        splits = 4
        step = pair_count // splits

        def product(start, token):
            held_cols, _ = lax.optimization_barrier((cols, token))
            return pair_products(place, me, held_cols, images, start, step)

        made = [functools.partial(product, i * step) for i in range(splits)]
        makers = {0: made[:1], 1: made[1:3], 2: made[3:]}
        diag_sum, made = sum_beside(diag, makers)
        kept = [keep for keep, _ in made]
        came = [swap(send, 1) for _, send in made]
        send = weigh(place, me, diag_sum, kept, came, sub_bits, False)
        across = swap(send, 1 << sub_bits)
        keep = weigh(place, me, diag_sum, kept, came, sub_bits, True)
        across, keep = lax.optimization_barrier((across, keep))
        own = reduce_pairs(keep + across.astype(F32), places, sub_bits)
        packed = own[None]
        for bit in range(sub_bits):
            packed = gather_bits(packed, 1, bit)
        share = rotation_share(0.01 / basis_count, me, packed)
        near, far = gather_pairs(share[None], sub_bits, pair_bits)
        if round_index + 1 < ROUNDS:
            earlier = rotate(place, me, near, cols, images, 0, ())
        else:
            turned = turn_near(place, me, near, cols)
        for bit in range(sub_bits):
            far = gather_bits(far, 1, bit)
        if round_index + 1 < ROUNDS:
            half = pair_count // 2
            cols, images, diag = rotate(place, me, far, cols, images, half, earlier)
    return rotate_last(place, matchings[ROUNDS - 1], me, turned, far, cols)


def solution(mesh):
    in_specs = (
        P("orb", "groups"),
        P("groups", "orb", None, None, None),
        P("orb", "groups"),
        P("groups", None),
    )
    out_specs = P("orb", "groups")
    return jax.shard_map(
        per_device, mesh=mesh, in_specs=in_specs, out_specs=out_specs, check_vma=False
    )
```

```python
import functools

import jax
import jax.numpy as jnp
from jax import lax
from jax.experimental import pallas as pl
from jax.experimental.pallas import tpu as pltpu
from jax.sharding import PartitionSpec as P

HALF = 128
BLK = 128
ROUNDS = 2
PAIR = 2 * HALF
F32 = jnp.float32
BF16 = jnp.bfloat16
VMEM_LIMIT = 24 * 1024 * 1024
VMEM = pl.BlockSpec(memory_space=pltpu.VMEM)
SMEM = pl.BlockSpec(memory_space=pltpu.SMEM)
TILE = 512
SMALL = 1e-6
WIRE = BF16


def params(limit=VMEM_LIMIT):
    return pltpu.CompilerParams(vmem_limit_bytes=limit)


def bits_of(count):
    return count.bit_length() - 1


def bitrev(value, bits):
    return sum(((value >> j) & 1) << (bits - 1 - j) for j in range(bits))


def swap(block, distance):
    count = lax.axis_size("orb")
    return lax.ppermute(block, "orb", [(i, i ^ distance) for i in range(count)])


def put_diag(diag_ref, component, block, cols, image, first):
    total = jnp.sum(cols.astype(F32) * image.astype(F32), axis=0, keepdims=True)
    for half in range(total.shape[1] // HALF):
        spot = pl.ds(block + half, 1)
        piece = total[:, half * HALF : (half + 1) * HALF]
        if first:
            diag_ref[component, spot, :] = piece
        else:
            diag_ref[component, spot, :] += piece


def edge_row_kernel(on_chip, me_ref, orbitals_ref, row_ref, sem):
    even = 1 - (me_ref[0] & 1)
    start = (even if on_chip else 1 - even) * (orbitals_ref.shape[0] - BLK)
    source = orbitals_ref.at[pl.ds(pl.multiple_of(start, BLK), BLK)]
    copy = pltpu.make_async_copy(source, row_ref, sem)
    copy.start()
    copy.wait()


def edge_row(me, orbitals, on_chip):
    return pl.pallas_call(
        functools.partial(edge_row_kernel, on_chip),
        out_shape=jax.ShapeDtypeStruct((BLK, orbitals.shape[1]), BF16),
        in_specs=[SMEM, pl.BlockSpec(memory_space=pltpu.HBM)],
        out_specs=VMEM,
        scratch_shapes=[pltpu.SemaphoreType.DMA],
        compiler_params=params(60 * 1024 * 1024),
        name="edge_row",
    )(me, orbitals)


def put_images(blocks_ref, cols_ref, window, b, tile, image_ref, diag_ref, first):
    out = jnp.dot(blocks_ref[b], window, preferred_element_type=F32).astype(BF16)
    own = cols_ref[b * BLK : (b + 1) * BLK, tile]
    for k in range(3):
        image = out[k * BLK : (k + 1) * BLK]
        image_ref[k, b * BLK : (b + 1) * BLK, tile] = image
        put_diag(diag_ref, k, tile.start // HALF, own, image, first)


def inner_kernel(block_rows, blocks_ref, cols_ref, image_ref, diag_ref):
    for start in range(0, cols_ref.shape[1], TILE):
        tile = slice(start, start + TILE)
        for b in range(1, block_rows - 1):
            window = cols_ref[(b - 1) * BLK : (b + 2) * BLK, tile]
            put_images(blocks_ref, cols_ref, window, b, tile, image_ref, diag_ref, b == 1)


def image_shapes(orbitals):
    row_count, orb_count = orbitals.shape
    return (
        jax.ShapeDtypeStruct((3, row_count, orb_count), BF16),
        jax.ShapeDtypeStruct((3, orb_count // HALF, HALF), F32),
    )


def inner_images(blocks, orbitals):
    return pl.pallas_call(
        functools.partial(inner_kernel, orbitals.shape[0] // BLK),
        out_shape=image_shapes(orbitals),
        in_specs=[VMEM, VMEM],
        out_specs=(VMEM, VMEM),
        compiler_params=params(),
        name="inner_images",
    )(blocks, orbitals)


def edge_kernel(
    block_rows, on_chip, me_ref, blocks_ref, cols_ref, came_ref, *refs
):
    old_diag_ref, image_ref, diag_ref = refs[1:]
    even = (me_ref[0] & 1) == 0
    last = even if on_chip else jnp.logical_not(even)
    diag_ref[...] = old_diag_ref[...]

    def put(b):
        for start in range(0, cols_ref.shape[1], TILE):
            tile = slice(start, start + TILE)
            if b == 0:
                pieces = [came_ref[:, tile], cols_ref[: 2 * BLK, tile]]
            else:
                pieces = [cols_ref[(b - 1) * BLK :, tile], came_ref[:, tile]]
            window = jnp.concatenate(pieces, axis=0)
            put_images(blocks_ref, cols_ref, window, b, tile, image_ref, diag_ref, False)

    @pl.when(last)
    def _():
        put(block_rows - 1)

    @pl.when(jnp.logical_not(last))
    def _():
        put(0)


def edge_images(me, blocks, orbitals, came, images, diag, on_chip):
    return pl.pallas_call(
        functools.partial(edge_kernel, orbitals.shape[0] // BLK, on_chip),
        out_shape=image_shapes(orbitals),
        in_specs=[SMEM] + [VMEM] * 5,
        out_specs=(VMEM, VMEM),
        input_output_aliases={4: 0, 5: 1},
        compiler_params=params(),
        name="edge_images",
    )(me, blocks, orbitals, came, images, diag)


def lower_mask():
    rows = lax.broadcasted_iota(jnp.int32, (HALF, HALF), 0)
    cols = lax.broadcasted_iota(jnp.int32, (HALF, HALF), 1)
    return rows > cols


def pair_columns(ref, lead, places):
    return jnp.concatenate(
        [ref[lead + (slice(None), pl.ds(pl.multiple_of(at * HALF, HALF), HALF))] for at in places],
        axis=1,
    )


def gram_kernel(first, place_ref, me_ref, cols_ref, image_ref, keep_ref, send_ref):
    mine = (me_ref[0] & 1) == 0
    low = lower_mask()
    for i in range(keep_ref.shape[0]):
        places = [place_ref[2 * (first + i) + h] for h in (0, 1)]
        cols = pair_columns(cols_ref, (), places)
        images = jnp.concatenate([pair_columns(image_ref, (k,), places) for k in range(3)], axis=1)
        mats = lax.dot_general(cols, images, (((0,), (0,)), ((), ())), preferred_element_type=F32)
        for k in range(3):
            mat = mats[:, k * PAIR : (k + 1) * PAIR]
            one, two = mat[:HALF, :HALF], mat[HALF:, HALF:]
            cross = mat[:HALF, HALF:] + mat[HALF:, :HALF].T
            within = jnp.where(low, one, two) + jnp.where(low, two, one).T
            keep_ref[i, k] = jnp.where(mine, cross, within)
            send_ref[i, k] = jnp.where(mine, within, cross)


def pair_products(place, me, cols, images, first, count):
    shape = jax.ShapeDtypeStruct((count, 3, HALF, HALF), F32)
    return pl.pallas_call(
        functools.partial(gram_kernel, first),
        out_shape=(shape, shape),
        in_specs=[SMEM, SMEM, VMEM, VMEM],
        out_specs=(VMEM, VMEM),
        compiler_params=params(),
        name="pair_products",
    )(place, me, cols, images)


def weight_kernel(sub_bits, stays, place_ref, me_ref, diag_ref, *refs):
    sums_refs, out_ref = refs[:-1], refs[-1]
    kept_refs, came_refs = sums_refs[: len(sums_refs) // 2], sums_refs[len(sums_refs) // 2 :]
    core = me_ref[0] & 1
    bit = (me_ref[0] >> sub_bits) & 1
    odd = bit if stays else 1 - bit
    rows = lax.broadcasted_iota(jnp.int32, (HALF, HALF), 0)
    cols = lax.broadcasted_iota(jnp.int32, (HALF, HALF), 1)
    low = jnp.where(rows > cols, 1, 0)
    col_first = jnp.maximum(low, 1 - core) > 0
    row_first = jnp.minimum(low, core) > 0
    step = kept_refs[0].shape[0]
    for j in range(out_ref.shape[0]):
        pair = 2 * j + odd
        i = 2 * j % step + odd
        kept_ref, came_ref = kept_refs[2 * j // step], came_refs[2 * j // step]
        halves = [
            [diag_ref[k, pl.ds(place_ref[2 * pair + h], 1), :] for k in range(3)] for h in (0, 1)
        ]
        first, second = [jnp.concatenate(half + half + half[:2], axis=0).T for half in halves]
        total = jnp.zeros((HALF, HALF), F32)
        for k in range(3):
            col = jnp.where(col_first, first[:, k : k + 1], second[:, k : k + 1])
            row = jnp.where(row_first, halves[0][k], halves[1][k])
            total += (kept_ref[i, k] + came_ref[i, k]) * (col - row)
        out_ref[j] = total.astype(out_ref.dtype)


def weigh(place, me, diag, kept, came, sub_bits, stays):
    high = sum(part.shape[0] for part in kept) // 2
    return pl.pallas_call(
        functools.partial(weight_kernel, sub_bits, stays),
        out_shape=jax.ShapeDtypeStruct((high, HALF, HALF), F32 if stays else BF16),
        in_specs=[SMEM, SMEM] + [VMEM] * (1 + 2 * len(kept)),
        out_specs=VMEM,
        compiler_params=params(),
        name="weigh",
    )(place, me, diag, *kept, *came)


def matmul(left, right):
    return jnp.dot(left, right, precision=lax.Precision.HIGHEST, preferred_element_type=F32)


def parts_of(value):
    high = value.astype(BF16)
    return high, (value - high.astype(F32)).astype(BF16)


def by_parts(left, right):
    left_high, left_low = parts_of(left)
    right_high, right_low = parts_of(right)
    rows = left.shape[0]
    both = jnp.dot(
        jnp.concatenate([left_high, left_low], axis=0), right_high, preferred_element_type=F32
    )
    return both[:rows] + (
        both[rows:] + jnp.dot(left_high, right_low, preferred_element_type=F32)
    )


def rotation_kernel(scale, subs, me_ref, packed_ref, out_ref, sum_ref, power_ref):
    sub = me_ref[0] & (subs - 1)
    pieces = [packed_ref[bitrev(i, bits_of(subs)) ^ sub] for i in range(subs)]
    packed = jnp.concatenate(pieces, axis=0) * scale
    cross, within = packed[:HALF], packed[HALF:]
    low = lower_mask()
    first = jnp.where(low, within, 0.0)
    second = jnp.where(low, 0.0, within)
    half_gen = jnp.concatenate(
        [
            jnp.concatenate([first - first.T, cross], axis=1),
            jnp.concatenate([-cross.T, second - second.T], axis=1),
        ],
        axis=0,
    )
    rows = lax.broadcasted_iota(jnp.int32, (PAIR, PAIR), 0)
    cols = lax.broadcasted_iota(jnp.int32, (PAIR, PAIR), 1)
    eye = jnp.where(rows == cols, 1.0, 0.0).astype(F32)

    def prepare(product):
        square = -product(half_gen, half_gen)
        fourth = product(square, square)
        bound = 1.0001 * jnp.sqrt(jnp.max(jnp.sum(jnp.abs(fourth), axis=1)))
        factor = 2.0 / (2.0 + bound)
        rest = 1.0 - factor
        sum_ref[...] = factor * ((1.0 + rest) * eye - factor * square)
        power_ref[...] = (
            rest * rest * eye - (2.0 * rest * factor) * square + factor * factor * fourth
        )
        return bound

    bound = prepare(by_parts)
    quick = bound < 16.0
    bound = lax.cond(quick, lambda: bound, lambda: prepare(matmul))

    def going(state):
        step, left = state
        return jnp.logical_and(step < 24, left > SMALL)

    def body(state):
        step, left = state
        power = power_ref[...]
        sum_ref[...] += matmul(sum_ref[...], power)

        @pl.when(left * left > SMALL)
        def _():
            power_ref[...] = matmul(power, power)

        return step + 1, left * left

    def quick_going(state):
        return jnp.logical_and(quick, going(state))

    def quick_body(state):
        step, left = state
        power = power_ref[...]
        both = by_parts(jnp.concatenate([sum_ref[...], power], axis=0), power)
        sum_ref[...] += both[:PAIR]
        power_ref[...] = both[PAIR:]
        return step + 1, left * left

    reach = bound / (2.0 + bound)
    state = lax.while_loop(quick_going, quick_body, (jnp.int32(0), reach * reach))
    lax.while_loop(going, body, state)
    share = PAIR // subs

    def finish(product):
        result = 2.0 * product(eye + half_gen, sum_ref[...]) - eye
        for i in range(subs):

            @pl.when(sub == i)
            def _():
                out_ref[...] = result[i * share : (i + 1) * share].astype(BF16)

    @pl.when(quick)
    def _():
        finish(by_parts)

    @pl.when(jnp.logical_not(quick))
    def _():
        finish(matmul)


def rotation_share(scale, me, packed):
    subs = packed.shape[0]
    return pl.pallas_call(
        functools.partial(rotation_kernel, scale, subs),
        out_shape=jax.ShapeDtypeStruct((PAIR // subs, PAIR), BF16),
        in_specs=[SMEM, VMEM],
        out_specs=VMEM,
        scratch_shapes=[pltpu.VMEM((PAIR, PAIR), F32), pltpu.VMEM((PAIR, PAIR), F32)],
        compiler_params=params(),
        name="rotation",
    )(me, packed)


def assemble(gathered_ref, me, slot):
    subs = PAIR // gathered_ref.shape[1]
    slots = gathered_ref.shape[0] // subs
    my_sub = me & (subs - 1)
    return jnp.concatenate(
        [gathered_ref[(i ^ my_sub) * slots + slot] for i in range(subs)], axis=0
    )


def rotate_kernel(first, place_ref, me_ref, gathered_ref, cols_ref, old_ref, *refs):
    subs = PAIR // gathered_ref.shape[1]
    my_pair = me_ref[0] // subs
    out_ref, image_ref, diag_ref = refs[-3:]
    for slot in range(gathered_ref.shape[0] // subs):
        p = my_pair ^ (first + slot)
        rotation = assemble(gathered_ref, me_ref[0], slot)
        places = [place_ref[2 * p + h] for h in (0, 1)]
        spot = pl.ds(pl.multiple_of(p * PAIR, PAIR), PAIR)
        cols = pair_columns(cols_ref, (), places)
        turned = jnp.dot(cols, rotation, preferred_element_type=F32).astype(BF16)
        out_ref[:, spot] = turned
        for k in range(3):
            image = pair_columns(old_ref, (k,), places)
            moved = jnp.dot(image, rotation, preferred_element_type=F32).astype(BF16)
            image_ref[k, :, spot] = moved
            put_diag(diag_ref, k, 2 * p, turned, moved, True)


def rotate(place, me, gathered, cols, images, first, earlier):
    row_count, orb_count = cols.shape
    operands = [place, me, gathered, cols, images]
    return pl.pallas_call(
        functools.partial(rotate_kernel, first),
        out_shape=(
            jax.ShapeDtypeStruct((row_count, orb_count), BF16),
            jax.ShapeDtypeStruct((3, row_count, orb_count), BF16),
            jax.ShapeDtypeStruct((3, orb_count // HALF, HALF), F32),
        ),
        in_specs=[SMEM, SMEM] + [VMEM] * (3 + len(earlier)),
        out_specs=(VMEM, VMEM, VMEM),
        cost_estimate=pl.CostEstimate(
            flops=8 * row_count * PAIR * PAIR * gathered.shape[0] * gathered.shape[1] // PAIR,
            bytes_accessed=8 * row_count * orb_count,
            transcendentals=0,
        ),
        input_output_aliases={len(operands) + i: i for i in range(len(earlier))},
        compiler_params=params(),
        name="rotate",
    )(*operands, *earlier)


def turn_kernel(place_ref, me_ref, gathered_ref, cols_ref, out_ref):
    subs = PAIR // gathered_ref.shape[1]
    for slot in range(gathered_ref.shape[0] // subs):
        p = (me_ref[0] // subs) ^ slot
        rotation = assemble(gathered_ref, me_ref[0], slot)
        cols = pair_columns(cols_ref, (), [place_ref[2 * p + h] for h in (0, 1)])
        turned = jnp.dot(cols, rotation, preferred_element_type=F32).astype(BF16)
        out_ref[:, slot * PAIR : (slot + 1) * PAIR] = turned


def turn_near(place, me, gathered, cols):
    row_count = cols.shape[0]
    subs = PAIR // gathered.shape[1]
    slots = gathered.shape[0] // subs
    return pl.pallas_call(
        turn_kernel,
        out_shape=jax.ShapeDtypeStruct((row_count, slots * PAIR), BF16),
        in_specs=[SMEM, SMEM, VMEM, VMEM],
        out_specs=VMEM,
        compiler_params=params(),
        name="turn_near",
    )(place, me, gathered, cols)


def last_kernel(
    place_ref, home_ref, me_ref, turned_ref, gathered_ref, cols_ref, out_ref, held_ref, sems
):
    subs = PAIR // gathered_ref.shape[1]
    near = turned_ref.shape[1] // PAIR
    copies = []
    for slot in range(near + gathered_ref.shape[0] // subs):
        p = (me_ref[0] // subs) ^ slot
        if slot < near:
            source_ref, start = turned_ref, slot * PAIR
        else:
            source_ref, start = held_ref, (slot - near) * PAIR
            rotation = assemble(gathered_ref, me_ref[0], slot - near)
            cols = pair_columns(cols_ref, (), [place_ref[2 * p + h] for h in (0, 1)])
            turned = jnp.dot(cols, rotation, preferred_element_type=F32).astype(BF16)
            held_ref[:, start : start + PAIR] = turned
        for h in (0, 1):
            home = pl.multiple_of(home_ref[2 * p + h] * HALF, HALF)
            copies.append(
                pltpu.make_async_copy(
                    source_ref.at[:, pl.ds(start + h * HALF, HALF)],
                    out_ref.at[:, pl.ds(home, HALF)],
                    sems.at[2 * slot + h],
                )
            )
            copies[-1].start()
    for copy in copies:
        copy.wait()


def rotate_last(place, home, me, turned, gathered, cols):
    row_count, orb_count = cols.shape
    return pl.pallas_call(
        last_kernel,
        out_shape=jax.ShapeDtypeStruct((row_count, orb_count), BF16),
        in_specs=[SMEM, SMEM, SMEM, VMEM, VMEM, VMEM],
        out_specs=pl.BlockSpec(memory_space=pltpu.HBM),
        scratch_shapes=[
            pltpu.VMEM((row_count, orb_count - turned.shape[1]), BF16),
            pltpu.SemaphoreType.DMA((orb_count // HALF,)),
        ],
        compiler_params=params(),
        name="rotate_last",
    )(place, home, me, turned, gathered, cols)


def sum_beside(diag, makers):
    made = []
    hops = bits_of(lax.axis_size("orb"))
    for bit in range(hops):
        arrived = swap(diag, 1 << bit)
        products, token = [], diag
        for maker in makers.get(bit, ()):
            products.append(maker(token))
            token = products[-1][0]
        diag, arrived, products = lax.optimization_barrier((diag, arrived, products))
        made += products
        diag = diag + arrived
    return diag, made


def places_of(position, sub_bits, pair_bits):
    steps = [(bit, 1) for bit in range(1, sub_bits)] + [(sub_bits + 1, pair_bits - 1)]
    found = {}
    for low_bit, bits in steps:
        mine = (position >> low_bit) & ((1 << bits) - 1)
        found[low_bit] = [(mine ^ q).astype(jnp.uint32) for q in range(1 << bits)]
    return found


def pick(value, at):
    zero = jnp.uint32(0)
    start = (at,) + (zero,) * (value.ndim - 1)
    return lax.dynamic_slice(value, start, (1,) + value.shape[1:])[0]


def spread(value, places, low_bit, wire):
    ways = len(places)
    value = value.reshape((ways, -1) + value.shape[1:])
    pieces = [
        swap(pick(value, places[q]).astype(wire), q << low_bit) for q in range(ways - 1, 0, -1)
    ]
    own = pick(value, places[0])
    for piece in pieces:
        own = own + piece.astype(F32)
    return own


def reduce_pairs(value, places, sub_bits):
    high = value.shape[0]
    for bit in range(1, sub_bits):
        rows = value.shape[1] // 2
        value = jnp.swapaxes(value.reshape(high, 2, rows, HALF), 0, 1)
        value = spread(value.reshape(2 * high, rows, HALF), places[bit], bit, F32)
    return spread(value, places[sub_bits + 1], sub_bits + 1, WIRE)[0]


def gather_bits(value, bits, low_bit):
    return jnp.concatenate(
        [value] + [swap(value, q << low_bit) for q in range(1, 1 << bits)], axis=0
    )


def gather_pairs(share, sub_bits, pair_bits):
    beside = 1 << sub_bits
    ways = 1 << (pair_bits - 1)
    away = {q: swap(share, q * 2 * beside) for q in range(ways - 1, 0, -1)}
    away[0] = share
    across = {q: swap(away[q], beside) for q in range(ways // 2)}
    across, away = lax.optimization_barrier((across, away))
    later = swap(jnp.concatenate([away[q] for q in range(ways // 2, ways)], axis=0), beside)
    near = jnp.concatenate([part[q] for q in range(ways // 2) for part in (away, across)], axis=0)
    for bit in range(sub_bits):
        near = gather_bits(near, 1, bit)
    later, near = lax.optimization_barrier((later, near))
    far = []
    for q in range(ways // 2, ways):
        far += [away[q], later[q - ways // 2 : q - ways // 2 + 1]]
    return near, jnp.concatenate(far, axis=0)


def per_device(orbitals, dipole_blocks, coupling_mask, matchings):
    row_count, orb_count = orbitals.shape
    count = lax.axis_size("orb")
    block_count = orb_count // HALF
    pair_count = orb_count // PAIR
    pair_bits = bits_of(pair_count)
    sub_bits = bits_of(count) - pair_bits
    basis_count = row_count * count
    block_rows = row_count // BLK
    position = lax.axis_index("orb").astype(jnp.int32)
    for_next = edge_row(position.reshape(1), orbitals, False)
    joints = [(i, i + 1) for i in range(1, count - 1, 2)]
    from_next = lax.ppermute(for_next, "orb", joints + [(j, i) for i, j in joints])
    orbitals, for_next = lax.optimization_barrier((orbitals, for_next))
    for_chip = edge_row(position.reshape(1), orbitals, True)
    from_chip = swap(for_chip, 1)
    orbitals, matchings, for_chip = lax.optimization_barrier((orbitals, matchings, for_chip))
    places = places_of(position, sub_bits, pair_bits)
    ident = jnp.arange(block_count, dtype=jnp.int32)
    held = [ident] + [matchings[r] for r in range(ROUNDS - 1)]
    spots = []
    for r in range(ROUNDS):
        found = jnp.where(matchings[r][:, None] == held[r][None, :], ident[None, :], 0)
        spots.append(jnp.sum(found, axis=1).astype(jnp.int32))
    orbitals, places, spots, me = lax.optimization_barrier(
        (orbitals, places, spots, position.reshape(1))
    )

    mask_full = jnp.stack(
        [coupling_mask[:, 0], jnp.ones((block_rows,), jnp.int32), coupling_mask[:, 1]], axis=1
    ).astype(BF16)
    blocks = jnp.transpose(
        dipole_blocks * mask_full[None, :, :, None, None], (1, 0, 3, 2, 4)
    ).reshape(block_rows, 3 * BLK, 3 * BLK)
    images, diag = inner_images(blocks, orbitals)
    images, diag = edge_images(me, blocks, orbitals, from_chip, images, diag, True)
    from_next, images, diag = lax.optimization_barrier((from_next, images, diag))
    images, diag = edge_images(me, blocks, orbitals, from_next, images, diag, False)
    cols = orbitals
    for round_index in range(ROUNDS):
        place = spots[round_index]
        splits = 4
        step = pair_count // splits

        def product(start, token):
            held_cols, _ = lax.optimization_barrier((cols, token))
            return pair_products(place, me, held_cols, images, start, step)

        made = [functools.partial(product, i * step) for i in range(splits)]
        makers = {0: made[:1], 1: made[1:3], 2: made[3:]}
        diag_sum, made = sum_beside(diag, makers)
        kept = [keep for keep, _ in made]
        came = [swap(send, 1) for _, send in made]
        send = weigh(place, me, diag_sum, kept, came, sub_bits, False)
        across = swap(send, 1 << sub_bits)
        keep = weigh(place, me, diag_sum, kept, came, sub_bits, True)
        across, keep = lax.optimization_barrier((across, keep))
        own = reduce_pairs(keep + across.astype(F32), places, sub_bits)
        packed = own[None]
        for bit in range(sub_bits):
            packed = gather_bits(packed, 1, bit)
        share = rotation_share(0.01 / basis_count, me, packed)
        near, far = gather_pairs(share[None], sub_bits, pair_bits)
        if round_index + 1 < ROUNDS:
            earlier = rotate(place, me, near, cols, images, 0, ())
        else:
            turned = turn_near(place, me, near, cols)
        for bit in range(sub_bits):
            far = gather_bits(far, 1, bit)
        if round_index + 1 < ROUNDS:
            half = pair_count // 2
            cols, images, diag = rotate(place, me, far, cols, images, half, earlier)
    return rotate_last(place, matchings[ROUNDS - 1], me, turned, far, cols)


def solution(mesh):
    in_specs = (
        P("orb", "groups"),
        P("groups", "orb", None, None, None),
        P("orb", "groups"),
        P("groups", None),
    )
    out_specs = P("orb", "groups")
    return jax.shard_map(
        per_device, mesh=mesh, in_specs=in_specs, out_specs=out_specs, check_vma=False
    )
```

```python
import functools

import jax
import jax.numpy as jnp
from jax import lax
from jax.experimental import pallas as pl
from jax.experimental.pallas import tpu as pltpu
from jax.sharding import PartitionSpec as P

HALF = 128
BLK = 128
ROUNDS = 2
PAIR = 2 * HALF
F32 = jnp.float32
BF16 = jnp.bfloat16
VMEM_LIMIT = 24 * 1024 * 1024
VMEM = pl.BlockSpec(memory_space=pltpu.VMEM)
SMEM = pl.BlockSpec(memory_space=pltpu.SMEM)
TILE = 512
SMALL = 1e-6
MIDDLE, LARGE = 16.0, 256.0
WIRE = BF16


def params(limit=VMEM_LIMIT):
    return pltpu.CompilerParams(vmem_limit_bytes=limit)


def bits_of(count):
    return count.bit_length() - 1


def bitrev(value, bits):
    return sum(((value >> j) & 1) << (bits - 1 - j) for j in range(bits))


def swap(block, distance):
    count = lax.axis_size("orb")
    return lax.ppermute(block, "orb", [(i, i ^ distance) for i in range(count)])


def put_diag(diag_ref, component, block, cols, image, first):
    total = jnp.sum(cols.astype(F32) * image.astype(F32), axis=0, keepdims=True)
    for half in range(total.shape[1] // HALF):
        spot = pl.ds(block + half, 1)
        piece = total[:, half * HALF : (half + 1) * HALF]
        if first:
            diag_ref[component, spot, :] = piece
        else:
            diag_ref[component, spot, :] += piece


def edge_row_kernel(on_chip, me_ref, orbitals_ref, row_ref, sem):
    even = 1 - (me_ref[0] & 1)
    start = (even if on_chip else 1 - even) * (orbitals_ref.shape[0] - BLK)
    source = orbitals_ref.at[pl.ds(pl.multiple_of(start, BLK), BLK)]
    copy = pltpu.make_async_copy(source, row_ref, sem)
    copy.start()
    copy.wait()


def edge_row(me, orbitals, on_chip):
    return pl.pallas_call(
        functools.partial(edge_row_kernel, on_chip),
        out_shape=jax.ShapeDtypeStruct((BLK, orbitals.shape[1]), BF16),
        in_specs=[SMEM, pl.BlockSpec(memory_space=pltpu.HBM)],
        out_specs=VMEM,
        scratch_shapes=[pltpu.SemaphoreType.DMA],
        compiler_params=params(60 * 1024 * 1024),
        name="edge_row",
    )(me, orbitals)


def put_images(blocks_ref, cols_ref, window, b, tile, image_ref, diag_ref, first):
    out = jnp.dot(blocks_ref[b], window, preferred_element_type=F32).astype(BF16)
    own = cols_ref[b * BLK : (b + 1) * BLK, tile]
    for k in range(3):
        image = out[k * BLK : (k + 1) * BLK]
        image_ref[k, b * BLK : (b + 1) * BLK, tile] = image
        put_diag(diag_ref, k, tile.start // HALF, own, image, first)


def inner_kernel(block_rows, blocks_ref, cols_ref, image_ref, diag_ref):
    for start in range(0, cols_ref.shape[1], TILE):
        tile = slice(start, start + TILE)
        for b in range(1, block_rows - 1):
            window = cols_ref[(b - 1) * BLK : (b + 2) * BLK, tile]
            put_images(blocks_ref, cols_ref, window, b, tile, image_ref, diag_ref, b == 1)


def image_shapes(orbitals):
    row_count, orb_count = orbitals.shape
    return (
        jax.ShapeDtypeStruct((3, row_count, orb_count), BF16),
        jax.ShapeDtypeStruct((3, orb_count // HALF, HALF), F32),
    )


def inner_images(blocks, orbitals):
    return pl.pallas_call(
        functools.partial(inner_kernel, orbitals.shape[0] // BLK),
        out_shape=image_shapes(orbitals),
        in_specs=[VMEM, VMEM],
        out_specs=(VMEM, VMEM),
        compiler_params=params(),
        name="inner_images",
    )(blocks, orbitals)


def edge_kernel(
    block_rows, on_chip, me_ref, blocks_ref, cols_ref, came_ref, *refs
):
    old_diag_ref, image_ref, diag_ref = refs[1:]
    even = (me_ref[0] & 1) == 0
    last = even if on_chip else jnp.logical_not(even)
    diag_ref[...] = old_diag_ref[...]

    def put(b):
        for start in range(0, cols_ref.shape[1], TILE):
            tile = slice(start, start + TILE)
            if b == 0:
                pieces = [came_ref[:, tile], cols_ref[: 2 * BLK, tile]]
            else:
                pieces = [cols_ref[(b - 1) * BLK :, tile], came_ref[:, tile]]
            window = jnp.concatenate(pieces, axis=0)
            put_images(blocks_ref, cols_ref, window, b, tile, image_ref, diag_ref, False)

    @pl.when(last)
    def _():
        put(block_rows - 1)

    @pl.when(jnp.logical_not(last))
    def _():
        put(0)


def edge_images(me, blocks, orbitals, came, images, diag, on_chip):
    return pl.pallas_call(
        functools.partial(edge_kernel, orbitals.shape[0] // BLK, on_chip),
        out_shape=image_shapes(orbitals),
        in_specs=[SMEM] + [VMEM] * 5,
        out_specs=(VMEM, VMEM),
        input_output_aliases={4: 0, 5: 1},
        compiler_params=params(),
        name="edge_images",
    )(me, blocks, orbitals, came, images, diag)


def lower_mask():
    rows = lax.broadcasted_iota(jnp.int32, (HALF, HALF), 0)
    cols = lax.broadcasted_iota(jnp.int32, (HALF, HALF), 1)
    return rows > cols


def pair_columns(ref, lead, places):
    return jnp.concatenate(
        [ref[lead + (slice(None), pl.ds(pl.multiple_of(at * HALF, HALF), HALF))] for at in places],
        axis=1,
    )


def gram_kernel(first, place_ref, me_ref, cols_ref, image_ref, keep_ref, send_ref):
    mine = (me_ref[0] & 1) == 0
    low = lower_mask()
    for i in range(keep_ref.shape[0]):
        places = [place_ref[2 * (first + i) + h] for h in (0, 1)]
        cols = pair_columns(cols_ref, (), places)
        images = jnp.concatenate([pair_columns(image_ref, (k,), places) for k in range(3)], axis=1)
        mats = lax.dot_general(cols, images, (((0,), (0,)), ((), ())), preferred_element_type=F32)
        for k in range(3):
            mat = mats[:, k * PAIR : (k + 1) * PAIR]
            one, two = mat[:HALF, :HALF], mat[HALF:, HALF:]
            cross = mat[:HALF, HALF:] + mat[HALF:, :HALF].T
            within = jnp.where(low, one, two) + jnp.where(low, two, one).T
            keep_ref[i, k] = jnp.where(mine, cross, within)
            send_ref[i, k] = jnp.where(mine, within, cross)


def pair_products(place, me, cols, images, first, count):
    shape = jax.ShapeDtypeStruct((count, 3, HALF, HALF), F32)
    return pl.pallas_call(
        functools.partial(gram_kernel, first),
        out_shape=(shape, shape),
        in_specs=[SMEM, SMEM, VMEM, VMEM],
        out_specs=(VMEM, VMEM),
        compiler_params=params(),
        name="pair_products",
    )(place, me, cols, images)


def weight_kernel(sub_bits, stays, place_ref, me_ref, diag_ref, *refs):
    sums_refs, out_ref = refs[:-1], refs[-1]
    kept_refs, came_refs = sums_refs[: len(sums_refs) // 2], sums_refs[len(sums_refs) // 2 :]
    core = me_ref[0] & 1
    bit = (me_ref[0] >> sub_bits) & 1
    odd = bit if stays else 1 - bit
    rows = lax.broadcasted_iota(jnp.int32, (HALF, HALF), 0)
    cols = lax.broadcasted_iota(jnp.int32, (HALF, HALF), 1)
    low = jnp.where(rows > cols, 1, 0)
    col_first = jnp.maximum(low, 1 - core) > 0
    row_first = jnp.minimum(low, core) > 0
    step = kept_refs[0].shape[0]
    for j in range(out_ref.shape[0]):
        pair = 2 * j + odd
        i = 2 * j % step + odd
        kept_ref, came_ref = kept_refs[2 * j // step], came_refs[2 * j // step]
        halves = [
            [diag_ref[k, pl.ds(place_ref[2 * pair + h], 1), :] for k in range(3)] for h in (0, 1)
        ]
        first, second = [jnp.concatenate(half + half + half[:2], axis=0).T for half in halves]
        total = jnp.zeros((HALF, HALF), F32)
        for k in range(3):
            col = jnp.where(col_first, first[:, k : k + 1], second[:, k : k + 1])
            row = jnp.where(row_first, halves[0][k], halves[1][k])
            total += (kept_ref[i, k] + came_ref[i, k]) * (col - row)
        out_ref[j] = total.astype(out_ref.dtype)


def weigh(place, me, diag, kept, came, sub_bits, stays):
    high = sum(part.shape[0] for part in kept) // 2
    return pl.pallas_call(
        functools.partial(weight_kernel, sub_bits, stays),
        out_shape=jax.ShapeDtypeStruct((high, HALF, HALF), F32 if stays else BF16),
        in_specs=[SMEM, SMEM] + [VMEM] * (1 + 2 * len(kept)),
        out_specs=VMEM,
        compiler_params=params(),
        name="weigh",
    )(place, me, diag, *kept, *came)


def matmul(left, right):
    return jnp.dot(left, right, precision=lax.Precision.HIGHEST, preferred_element_type=F32)


def parts_of(value):
    high = value.astype(BF16)
    return high, (value - high.astype(F32)).astype(BF16)


def by_parts(left, right):
    left_high, left_low = parts_of(left)
    right_high, right_low = parts_of(right)
    rows = left.shape[0]
    both = jnp.dot(
        jnp.concatenate([left_high, left_low], axis=0), right_high, preferred_element_type=F32
    )
    return both[:rows] + (
        both[rows:] + jnp.dot(left_high, right_low, preferred_element_type=F32)
    )


def rotation_kernel(scale, subs, me_ref, packed_ref, out_ref, sum_ref, power_ref):
    sub = me_ref[0] & (subs - 1)
    pieces = [packed_ref[bitrev(i, bits_of(subs)) ^ sub] for i in range(subs)]
    packed = jnp.concatenate(pieces, axis=0) * scale
    cross, within = packed[:HALF], packed[HALF:]
    low = lower_mask()
    first = jnp.where(low, within, 0.0)
    second = jnp.where(low, 0.0, within)
    half_gen = jnp.concatenate(
        [
            jnp.concatenate([first - first.T, cross], axis=1),
            jnp.concatenate([-cross.T, second - second.T], axis=1),
        ],
        axis=0,
    )
    rows = lax.broadcasted_iota(jnp.int32, (PAIR, PAIR), 0)
    cols = lax.broadcasted_iota(jnp.int32, (PAIR, PAIR), 1)
    eye = jnp.where(rows == cols, 1.0, 0.0).astype(F32)

    def prepare(product):
        square = -product(half_gen, half_gen)
        fourth = product(square, square)
        bound = 1.0001 * jnp.sqrt(jnp.max(jnp.sum(jnp.abs(fourth), axis=1)))
        factor = 2.0 / (2.0 + bound)
        rest = 1.0 - factor
        sum_ref[...] = factor * ((1.0 + rest) * eye - factor * square)
        power_ref[...] = (
            rest * rest * eye - (2.0 * rest * factor) * square + factor * factor * fourth
        )
        return bound

    bound = prepare(by_parts)
    quick = bound < LARGE
    bound = lax.cond(quick, lambda: bound, lambda: prepare(matmul))

    def going(state):
        step, left = state
        return jnp.logical_and(step < 24, left > SMALL)

    def body(state):
        step, left = state
        power = power_ref[...]
        sum_ref[...] += matmul(sum_ref[...], power)

        @pl.when(left * left > SMALL)
        def _():
            power_ref[...] = matmul(power, power)

        return step + 1, left * left

    def quick_going(state):
        return jnp.logical_and(quick, going(state))

    def quick_body(state):
        step, left = state
        power = power_ref[...]
        both = by_parts(jnp.concatenate([sum_ref[...], power], axis=0), power)
        sum_ref[...] += both[:PAIR]
        power_ref[...] = both[PAIR:]
        return step + 1, left * left

    reach = bound / (2.0 + bound)
    state = lax.while_loop(quick_going, quick_body, (jnp.int32(0), reach * reach))
    lax.while_loop(going, body, state)

    @pl.when(jnp.logical_and(quick, bound >= MIDDLE))
    def _():
        inverse = sum_ref[...]
        missing = eye - inverse + matmul(matmul(half_gen, half_gen), inverse)
        sum_ref[...] = inverse + by_parts(inverse, missing)

    share = PAIR // subs

    def finish(product):
        result = 2.0 * product(eye + half_gen, sum_ref[...]) - eye
        for i in range(subs):

            @pl.when(sub == i)
            def _():
                out_ref[...] = result[i * share : (i + 1) * share].astype(BF16)

    @pl.when(quick)
    def _():
        finish(by_parts)

    @pl.when(jnp.logical_not(quick))
    def _():
        finish(matmul)


def rotation_share(scale, me, packed):
    subs = packed.shape[0]
    return pl.pallas_call(
        functools.partial(rotation_kernel, scale, subs),
        out_shape=jax.ShapeDtypeStruct((PAIR // subs, PAIR), BF16),
        in_specs=[SMEM, VMEM],
        out_specs=VMEM,
        scratch_shapes=[pltpu.VMEM((PAIR, PAIR), F32), pltpu.VMEM((PAIR, PAIR), F32)],
        compiler_params=params(),
        name="rotation",
    )(me, packed)


def assemble(gathered_ref, me, slot):
    subs = PAIR // gathered_ref.shape[1]
    slots = gathered_ref.shape[0] // subs
    my_sub = me & (subs - 1)
    return jnp.concatenate(
        [gathered_ref[(i ^ my_sub) * slots + slot] for i in range(subs)], axis=0
    )


def rotate_kernel(first, place_ref, me_ref, gathered_ref, cols_ref, old_ref, *refs):
    subs = PAIR // gathered_ref.shape[1]
    my_pair = me_ref[0] // subs
    out_ref, image_ref, diag_ref = refs[-3:]
    for slot in range(gathered_ref.shape[0] // subs):
        p = my_pair ^ (first + slot)
        rotation = assemble(gathered_ref, me_ref[0], slot)
        places = [place_ref[2 * p + h] for h in (0, 1)]
        spot = pl.ds(pl.multiple_of(p * PAIR, PAIR), PAIR)
        cols = pair_columns(cols_ref, (), places)
        turned = jnp.dot(cols, rotation, preferred_element_type=F32).astype(BF16)
        out_ref[:, spot] = turned
        for k in range(3):
            image = pair_columns(old_ref, (k,), places)
            moved = jnp.dot(image, rotation, preferred_element_type=F32).astype(BF16)
            image_ref[k, :, spot] = moved
            put_diag(diag_ref, k, 2 * p, turned, moved, True)


def rotate(place, me, gathered, cols, images, first, earlier):
    row_count, orb_count = cols.shape
    operands = [place, me, gathered, cols, images]
    return pl.pallas_call(
        functools.partial(rotate_kernel, first),
        out_shape=(
            jax.ShapeDtypeStruct((row_count, orb_count), BF16),
            jax.ShapeDtypeStruct((3, row_count, orb_count), BF16),
            jax.ShapeDtypeStruct((3, orb_count // HALF, HALF), F32),
        ),
        in_specs=[SMEM, SMEM] + [VMEM] * (3 + len(earlier)),
        out_specs=(VMEM, VMEM, VMEM),
        cost_estimate=pl.CostEstimate(
            flops=8 * row_count * PAIR * PAIR * gathered.shape[0] * gathered.shape[1] // PAIR,
            bytes_accessed=8 * row_count * orb_count,
            transcendentals=0,
        ),
        input_output_aliases={len(operands) + i: i for i in range(len(earlier))},
        compiler_params=params(),
        name="rotate",
    )(*operands, *earlier)


def turn_kernel(place_ref, me_ref, gathered_ref, cols_ref, out_ref):
    subs = PAIR // gathered_ref.shape[1]
    for slot in range(gathered_ref.shape[0] // subs):
        p = (me_ref[0] // subs) ^ slot
        rotation = assemble(gathered_ref, me_ref[0], slot)
        cols = pair_columns(cols_ref, (), [place_ref[2 * p + h] for h in (0, 1)])
        turned = jnp.dot(cols, rotation, preferred_element_type=F32).astype(BF16)
        out_ref[:, slot * PAIR : (slot + 1) * PAIR] = turned


def turn_near(place, me, gathered, cols):
    row_count = cols.shape[0]
    subs = PAIR // gathered.shape[1]
    slots = gathered.shape[0] // subs
    return pl.pallas_call(
        turn_kernel,
        out_shape=jax.ShapeDtypeStruct((row_count, slots * PAIR), BF16),
        in_specs=[SMEM, SMEM, VMEM, VMEM],
        out_specs=VMEM,
        compiler_params=params(),
        name="turn_near",
    )(place, me, gathered, cols)


def last_kernel(
    place_ref, home_ref, me_ref, turned_ref, gathered_ref, cols_ref, out_ref, held_ref, sems
):
    subs = PAIR // gathered_ref.shape[1]
    near = turned_ref.shape[1] // PAIR
    copies = []
    for slot in range(near + gathered_ref.shape[0] // subs):
        p = (me_ref[0] // subs) ^ slot
        if slot < near:
            source_ref, start = turned_ref, slot * PAIR
        else:
            source_ref, start = held_ref, (slot - near) * PAIR
            rotation = assemble(gathered_ref, me_ref[0], slot - near)
            cols = pair_columns(cols_ref, (), [place_ref[2 * p + h] for h in (0, 1)])
            turned = jnp.dot(cols, rotation, preferred_element_type=F32).astype(BF16)
            held_ref[:, start : start + PAIR] = turned
        for h in (0, 1):
            home = pl.multiple_of(home_ref[2 * p + h] * HALF, HALF)
            copies.append(
                pltpu.make_async_copy(
                    source_ref.at[:, pl.ds(start + h * HALF, HALF)],
                    out_ref.at[:, pl.ds(home, HALF)],
                    sems.at[2 * slot + h],
                )
            )
            copies[-1].start()
    for copy in copies:
        copy.wait()


def rotate_last(place, home, me, turned, gathered, cols):
    row_count, orb_count = cols.shape
    return pl.pallas_call(
        last_kernel,
        out_shape=jax.ShapeDtypeStruct((row_count, orb_count), BF16),
        in_specs=[SMEM, SMEM, SMEM, VMEM, VMEM, VMEM],
        out_specs=pl.BlockSpec(memory_space=pltpu.HBM),
        scratch_shapes=[
            pltpu.VMEM((row_count, orb_count - turned.shape[1]), BF16),
            pltpu.SemaphoreType.DMA((orb_count // HALF,)),
        ],
        compiler_params=params(),
        name="rotate_last",
    )(place, home, me, turned, gathered, cols)


def sum_beside(diag, makers):
    made = []
    hops = bits_of(lax.axis_size("orb"))
    for bit in range(hops):
        arrived = swap(diag, 1 << bit)
        products, token = [], diag
        for maker in makers.get(bit, ()):
            products.append(maker(token))
            token = products[-1][0]
        diag, arrived, products = lax.optimization_barrier((diag, arrived, products))
        made += products
        diag = diag + arrived
    return diag, made


def places_of(position, sub_bits, pair_bits):
    steps = [(bit, 1) for bit in range(1, sub_bits)] + [(sub_bits + 1, pair_bits - 1)]
    found = {}
    for low_bit, bits in steps:
        mine = (position >> low_bit) & ((1 << bits) - 1)
        found[low_bit] = [(mine ^ q).astype(jnp.uint32) for q in range(1 << bits)]
    return found


def pick(value, at):
    zero = jnp.uint32(0)
    start = (at,) + (zero,) * (value.ndim - 1)
    return lax.dynamic_slice(value, start, (1,) + value.shape[1:])[0]


def spread(value, places, low_bit, wire):
    ways = len(places)
    value = value.reshape((ways, -1) + value.shape[1:])
    pieces = [
        swap(pick(value, places[q]).astype(wire), q << low_bit) for q in range(ways - 1, 0, -1)
    ]
    own = pick(value, places[0])
    for piece in pieces:
        own = own + piece.astype(F32)
    return own


def reduce_pairs(value, places, sub_bits):
    high = value.shape[0]
    for bit in range(1, sub_bits):
        rows = value.shape[1] // 2
        value = jnp.swapaxes(value.reshape(high, 2, rows, HALF), 0, 1)
        value = spread(value.reshape(2 * high, rows, HALF), places[bit], bit, F32)
    return spread(value, places[sub_bits + 1], sub_bits + 1, WIRE)[0]


def gather_bits(value, bits, low_bit):
    return jnp.concatenate(
        [value] + [swap(value, q << low_bit) for q in range(1, 1 << bits)], axis=0
    )


def gather_pairs(share, sub_bits, pair_bits):
    beside = 1 << sub_bits
    ways = 1 << (pair_bits - 1)
    away = {q: swap(share, q * 2 * beside) for q in range(ways - 1, 0, -1)}
    away[0] = share
    across = {q: swap(away[q], beside) for q in range(ways // 2)}
    across, away = lax.optimization_barrier((across, away))
    later = swap(jnp.concatenate([away[q] for q in range(ways // 2, ways)], axis=0), beside)
    near = jnp.concatenate([part[q] for q in range(ways // 2) for part in (away, across)], axis=0)
    for bit in range(sub_bits):
        near = gather_bits(near, 1, bit)
    later, near = lax.optimization_barrier((later, near))
    far = []
    for q in range(ways // 2, ways):
        far += [away[q], later[q - ways // 2 : q - ways // 2 + 1]]
    return near, jnp.concatenate(far, axis=0)


def per_device(orbitals, dipole_blocks, coupling_mask, matchings):
    row_count, orb_count = orbitals.shape
    count = lax.axis_size("orb")
    block_count = orb_count // HALF
    pair_count = orb_count // PAIR
    pair_bits = bits_of(pair_count)
    sub_bits = bits_of(count) - pair_bits
    basis_count = row_count * count
    block_rows = row_count // BLK
    position = lax.axis_index("orb").astype(jnp.int32)
    for_next = edge_row(position.reshape(1), orbitals, False)
    joints = [(i, i + 1) for i in range(1, count - 1, 2)]
    from_next = lax.ppermute(for_next, "orb", joints + [(j, i) for i, j in joints])
    orbitals, for_next = lax.optimization_barrier((orbitals, for_next))
    for_chip = edge_row(position.reshape(1), orbitals, True)
    from_chip = swap(for_chip, 1)
    orbitals, matchings, for_chip = lax.optimization_barrier((orbitals, matchings, for_chip))
    places = places_of(position, sub_bits, pair_bits)
    ident = jnp.arange(block_count, dtype=jnp.int32)
    held = [ident] + [matchings[r] for r in range(ROUNDS - 1)]
    spots = []
    for r in range(ROUNDS):
        found = jnp.where(matchings[r][:, None] == held[r][None, :], ident[None, :], 0)
        spots.append(jnp.sum(found, axis=1).astype(jnp.int32))
    orbitals, places, spots, me = lax.optimization_barrier(
        (orbitals, places, spots, position.reshape(1))
    )

    mask_full = jnp.stack(
        [coupling_mask[:, 0], jnp.ones((block_rows,), jnp.int32), coupling_mask[:, 1]], axis=1
    ).astype(BF16)
    blocks = jnp.transpose(
        dipole_blocks * mask_full[None, :, :, None, None], (1, 0, 3, 2, 4)
    ).reshape(block_rows, 3 * BLK, 3 * BLK)
    images, diag = inner_images(blocks, orbitals)
    images, diag = edge_images(me, blocks, orbitals, from_chip, images, diag, True)
    from_next, images, diag = lax.optimization_barrier((from_next, images, diag))
    images, diag = edge_images(me, blocks, orbitals, from_next, images, diag, False)
    cols = orbitals
    for round_index in range(ROUNDS):
        place = spots[round_index]
        splits = 4
        step = pair_count // splits

        def product(start, token):
            held_cols, _ = lax.optimization_barrier((cols, token))
            return pair_products(place, me, held_cols, images, start, step)

        made = [functools.partial(product, i * step) for i in range(splits)]
        makers = {0: made[:1], 1: made[1:3], 2: made[3:]}
        diag_sum, made = sum_beside(diag, makers)
        kept = [keep for keep, _ in made]
        came = [swap(send, 1) for _, send in made]
        send = weigh(place, me, diag_sum, kept, came, sub_bits, False)
        across = swap(send, 1 << sub_bits)
        keep = weigh(place, me, diag_sum, kept, came, sub_bits, True)
        across, keep = lax.optimization_barrier((across, keep))
        own = reduce_pairs(keep + across.astype(F32), places, sub_bits)
        packed = own[None]
        for bit in range(sub_bits):
            packed = gather_bits(packed, 1, bit)
        share = rotation_share(0.01 / basis_count, me, packed)
        near, far = gather_pairs(share[None], sub_bits, pair_bits)
        if round_index + 1 < ROUNDS:
            earlier = rotate(place, me, near, cols, images, 0, ())
        else:
            turned = turn_near(place, me, near, cols)
        for bit in range(sub_bits):
            far = gather_bits(far, 1, bit)
        if round_index + 1 < ROUNDS:
            half = pair_count // 2
            cols, images, diag = rotate(place, me, far, cols, images, half, earlier)
    return rotate_last(place, matchings[ROUNDS - 1], me, turned, far, cols)


def solution(mesh):
    in_specs = (
        P("orb", "groups"),
        P("groups", "orb", None, None, None),
        P("orb", "groups"),
        P("groups", None),
    )
    out_specs = P("orb", "groups")
    return jax.shard_map(
        per_device, mesh=mesh, in_specs=in_specs, out_specs=out_specs, check_vma=False
    )
```
